512 devices in a mesh: bx: 32 (over x, y_lo, core), by: 16 (over z, y_hi).
Axes of the slice: x: 4, y: 8 (y_hi: 2, y_lo: 4; y = y_hi * 4 + y_lo), z: 8, core: 2. Of those that a mesh axis runs over, the one named last changes fastest.
Arguments:
- weights: float32 [2, 25, 128, 128, 128], P(None, None, 'bx', 'by'), may hold values from -6 to 6
Outputs:
- radon_data: float32 [8, 2, 32, 64], P(None, None, 'bx', 'by')
The draws below stay inside these ranges and needn't reach their ends.
All inputs are finite; a program needn't handle non-finite values.
Results may differ from the reference program's by a relative error of at most 0.0013.
Values sent between devices are 32-bit elements; how exact they have to be, the bound alone decides.
A program may use at most 128 MiB of HBM per device.

```python
import math
import jax
import jax.numpy as jnp
import numpy as np
from jax import lax

N = 16384
P_SIZE = 5
LEVEL_BOXES = 128
EV = 8
TXD = 1
TYD = 4
SX_DEV = 4
SY_DEV = 8
TGT = 128
N_BX = 32
N_BY = 16


def block_scale(own_key, shape, shards, smallest, top_value):
    factor_of = 1.0
    for axis_at, shards_of in shards:
        steps = jax.random.uniform(jax.random.fold_in(jax.random.fold_in(own_key, 6), axis_at), (shards_of,), jnp.float32, smallest / len(shards), top_value / len(shards))
        factor_of = factor_of * jnp.repeat(jnp.exp(steps), shape[axis_at] // shards_of).reshape((-1,) + (1,) * (len(shape) - 1 - axis_at))
    return factor_of


def normal_values(stream_key, dims, deviation, limit, shards=(), kind=jnp.bfloat16):
    values = jax.random.normal(stream_key, dims, jnp.float32) * deviation
    if len(shards) > 0:
        values = block_scale(stream_key, dims, shards, -0.22, 0.18) * values
    return jnp.clip(values, min=-limit, max=limit).astype(kind)


def setup_inputs(seed: int = 0) -> dict:
    arg_keys = jax.random.split(jax.random.key(seed), 2)
    weights = normal_values(arg_keys[0], (2, P_SIZE * P_SIZE, LEVEL_BOXES, LEVEL_BOXES, TGT), 1.0, 6.0, ((2, 32), (3, 16)), jnp.float32)
    return {"weights": weights}


TWO_PI = 2.0 * math.pi

def node_values():
    return np.cos(np.pi * (2.0 * np.arange(P_SIZE) + 1.0) / (2.0 * P_SIZE)) / 2.0

def lagrange_tables(direction):
    node_vals = node_values()
    stacked = []
    for child_no in range(2):
        child_nodes = (child_no - 0.5) / 2.0 + node_vals / 2.0
        factor = np.ones((P_SIZE, P_SIZE))
        for basis_no in range(P_SIZE):
            for other_no in range(P_SIZE):
                if other_no != basis_no:
                    factor[basis_no, :] = factor[basis_no, :] * (child_nodes - node_vals[other_no]) / (node_vals[basis_no] - node_vals[other_no])
        if direction == 0:
            stacked.append(np.kron(factor, np.eye(P_SIZE)))
        else:
            stacked.append(np.kron(np.eye(P_SIZE), factor))
    return jnp.asarray(np.stack(stacked), dtype=jnp.float32)

def node_offsets():
    node_vals = node_values()
    return (jnp.asarray(np.repeat(node_vals, P_SIZE), dtype=jnp.float32), jnp.asarray(np.tile(node_vals, P_SIZE), dtype=jnp.float32))

def point_offsets():
    step_list = np.arange(EV)
    across = (step_list + 0.5) / EV - 0.5
    upward = (3 * step_list % EV + 0.5) / EV - 0.5
    return jnp.asarray(np.stack([across, upward], axis=1), dtype=jnp.float32)

def box_centers(index_values, width):
    return -N / 2.0 + width * (index_values + 0.5)

def target_lines(count_x, count_y):
    column_ids = (17 * jnp.arange(count_x, dtype=jnp.int32) + 3) % LEVEL_BOXES
    row_ids = (29 * jnp.arange(count_y, dtype=jnp.int32) + 11) % LEVEL_BOXES
    return ((column_ids.astype(jnp.float32) + 0.5) / LEVEL_BOXES, (row_ids.astype(jnp.float32) + 0.5) / LEVEL_BOXES)

def speeds(pos_x, pos_y):
    wave_x = jnp.sin(TWO_PI * pos_x) * jnp.sin(TWO_PI * pos_y)
    wave_y = jnp.cos(TWO_PI * pos_x) * jnp.cos(TWO_PI * pos_y)
    return ((2.0 + wave_x) / 16.0, (2.0 + wave_y) / 16.0)

def relative(pos_x, pos_y, off_x, off_y, ref_x, ref_y):
    speed_x, speed_y = speeds(pos_x, pos_y)
    square_x = speed_x * speed_x
    square_y = speed_y * speed_y
    freq_x = ref_x + off_x
    freq_y = ref_y + off_y
    norm_freq = jnp.sqrt(square_x * freq_x * freq_x + square_y * freq_y * freq_y)
    norm_ref = jnp.sqrt(square_x * ref_x * ref_x + square_y * ref_y * ref_y)
    upper_term = square_x * off_x * (freq_x + ref_x) + square_y * off_y * (freq_y + ref_y)
    return pos_x * off_x + pos_y * off_y + upper_term / (norm_freq + norm_ref)

def moving(new_x, new_y, old_x, old_y, freq_x, freq_y):
    fresh_x, fresh_y = speeds(new_x, new_y)
    stale_x, stale_y = speeds(old_x, old_y)
    upper_term = (fresh_x - stale_x) * (fresh_x + stale_x) * freq_x * freq_x + (fresh_y - stale_y) * (fresh_y + stale_y) * freq_y * freq_y
    norm_new = jnp.sqrt(fresh_x * fresh_x * freq_x * freq_x + fresh_y * fresh_y * freq_y * freq_y)
    norm_old = jnp.sqrt(stale_x * stale_x * freq_x * freq_x + stale_y * stale_y * freq_y * freq_y)
    return (new_x - old_x) * freq_x + (new_y - old_y) * freq_y + upper_term / (norm_new + norm_old)

def rotate(current, phases, sign):
    cosine = jnp.cos(TWO_PI * phases)
    sine_part = sign * jnp.sin(TWO_PI * phases)
    return jnp.stack([current[0] * cosine - current[1] * sine_part, current[0] * sine_part + current[1] * cosine])

def child_term(current, factor, new_x, new_y, old_x, old_y, cen_x, cen_y, width_x, width_y):
    leading, trailing = node_offsets()
    off_x = (leading * width_x)[:, None, None, None]
    off_y = (trailing * width_y)[:, None, None, None]
    ref_x = cen_x[None, :, None, None]
    ref_y = cen_y[None, None, :, None]
    pos_x = new_x[None, None, None, :]
    pos_y = new_y[None, None, None, :]
    phases = relative(pos_x, pos_y, off_x, off_y, ref_x, ref_y) + moving(pos_x, pos_y, old_x[None, None, None, :], old_y[None, None, None, :], ref_x, ref_y)
    turned = rotate(current, phases, 1.0)
    return jnp.einsum('ab,rbxyn->raxyn', factor, turned, precision=lax.Precision.HIGHEST)

def parent_phase(summed, new_x, new_y, cen_x, cen_y, width_x, width_y):
    leading, trailing = node_offsets()
    phases = relative(new_x[None, None, None, :], new_y[None, None, None, :], (leading * width_x)[:, None, None, None], (trailing * width_y)[:, None, None, None], cen_x[None, :, None, None], cen_y[None, None, :, None])
    return rotate(summed, phases, -1.0)

def evaluate(current, tgt_x, tgt_y, cen_x, cen_y, width_x, width_y, box_width):
    leading, trailing = node_offsets()
    off_x = (leading * width_x)[:, None, None, None]
    off_y = (trailing * width_y)[:, None, None, None]
    ref_x = cen_x[None, :, None, None]
    ref_y = cen_y[None, None, :, None]
    center_x = tgt_x[None, None, None, :]
    center_y = tgt_y[None, None, None, :]

    def one_point(offset):
        pos_x = (tgt_x + offset[0] * box_width)[None, None, None, :]
        pos_y = (tgt_y + offset[1] * box_width)[None, None, None, :]
        phases = relative(pos_x, pos_y, off_x, off_y, ref_x, ref_y) + moving(pos_x, pos_y, center_x, center_y, ref_x, ref_y)
        return lax.optimization_barrier(jnp.sum(rotate(current, phases, 1.0), axis=(1, 2, 3)))
    return lax.map(one_point, point_offsets())

def arrange(direction, new_pos, targets, moving_centers, fixed_centers):
    if direction == 0:
        return (new_pos, targets[1], moving_centers, fixed_centers)
    return (targets[0], new_pos, fixed_centers, moving_centers)

def split_pairs(current, direction, targets, src_widths, tgt_widths):
    tables = lagrange_tables(direction)
    child_width = src_widths[direction]
    box_count = current.shape[2 + direction] // 2
    fixed_count = current.shape[3 - direction]
    par_centers = box_centers(jnp.arange(box_count, dtype=jnp.float32), 2.0 * child_width)
    fixed_centers = box_centers(jnp.arange(fixed_count, dtype=jnp.float32), src_widths[1 - direction])
    if direction == 0:
        pieces = current.reshape(2, P_SIZE * P_SIZE, box_count, 2, fixed_count, -1)
        children = [pieces[:, :, :, 0], pieces[:, :, :, 1]]
    else:
        pieces = current.reshape(2, P_SIZE * P_SIZE, fixed_count, box_count, 2, -1)
        children = [pieces[:, :, :, :, 0], pieces[:, :, :, :, 1]]
    parent_widths = [src_widths[0], src_widths[1]]
    parent_widths[direction] = 2.0 * child_width
    step_size = tgt_widths[direction] / 2.0
    results = []
    new_lines = []
    for target_no in range(2):
        new_pos = targets[direction] + (target_no - 0.5) * step_size
        child_terms = []
        for child_no in range(2):
            child_center = par_centers + (child_no - 0.5) * child_width
            new_x, new_y, cen_x, cen_y = arrange(direction, new_pos, targets, child_center, fixed_centers)
            child_terms.append(child_term(children[child_no], tables[child_no], new_x, new_y, targets[0], targets[1], cen_x, cen_y, src_widths[0], src_widths[1]))
        summed = child_terms[0] + child_terms[1]
        new_x, new_y, cen_x, cen_y = arrange(direction, new_pos, targets, par_centers, fixed_centers)
        results.append(parent_phase(summed, new_x, new_y, cen_x, cen_y, parent_widths[0], parent_widths[1]))
        new_lines.append(new_pos)
    renewed = jnp.stack(results, axis=-1)
    renewed = renewed.reshape(2, P_SIZE * P_SIZE, renewed.shape[2], renewed.shape[3], -1)
    split_line = jnp.stack(new_lines, axis=-1).reshape(-1)
    if direction == 0:
        return (renewed, [split_line, jnp.repeat(targets[1], 2)])
    return (renewed, [jnp.repeat(targets[0], 2), split_line])

def reference(weights):
    count_x = TXD * N_BX // 4
    count_y = TYD * N_BY // 4
    line_x, line_y = target_lines(count_x, count_y)
    blocks = weights.reshape(2, P_SIZE * P_SIZE, N_BX, SX_DEV, N_BY, SY_DEV, count_x, count_y)
    blocks = jnp.transpose(blocks, (7, 0, 1, 3, 2, 5, 4, 6)).reshape(count_y, 2, P_SIZE * P_SIZE, LEVEL_BOXES, LEVEL_BOXES, count_x)

    def one_row(inputs):
        current, row_pos = inputs
        targets = [line_x, jnp.zeros((count_x,), jnp.float32) + row_pos]
        src_widths = [N / LEVEL_BOXES, N / LEVEL_BOXES]
        tgt_widths = [1.0 / LEVEL_BOXES, 1.0 / LEVEL_BOXES]
        for level_no in range(2):
            for direction in range(2):
                current, targets = split_pairs(current, direction, targets, src_widths, tgt_widths)
                src_widths[direction] = 2.0 * src_widths[direction]
                tgt_widths[direction] = tgt_widths[direction] / 2.0
        final_x = box_centers(jnp.arange(current.shape[2], dtype=jnp.float32), src_widths[0])
        final_y = box_centers(jnp.arange(current.shape[3], dtype=jnp.float32), src_widths[1])
        return evaluate(current, targets[0], targets[1], final_x, final_y, src_widths[0], src_widths[1], tgt_widths[0])
    row_parts = lax.map(one_row, (blocks, line_y))
    row_parts = row_parts.reshape(N_BY // 4, TYD, EV, 2, N_BX // 4, TXD, 2, 2, 2, 2)
    row_parts = jnp.transpose(row_parts, (2, 3, 4, 8, 6, 5, 0, 9, 7, 1))
    return row_parts.reshape(EV, 2, N_BX * TXD, N_BY * TYD) * (1.0 / (P_SIZE * LEVEL_BOXES))
```

```python
import functools
import math

import jax
import jax.numpy as jnp
import numpy as np
from jax import lax
from jax.experimental import pallas as pl
from jax.experimental.pallas import tpu as pltpu
from jax.sharding import PartitionSpec as P

N = 16384
P_SIZE = 5
LEVEL_BOXES = 128
EV = 8
NODES = P_SIZE * P_SIZE
ROWS = 2 * NODES
SLOT = 104
FIRST = 56
MESH = pl.DeviceIdType.MESH

SIN = (4.44288292, -7.3082457, 3.60635441, -0.84611289, 0.10982699)
COS = (1.4142135, -6.97885099, 5.73946117, -1.88356299, 0.31069819)


def nodes():
    return np.cos(np.pi * (2.0 * np.arange(P_SIZE) + 1.0) / (2.0 * P_SIZE)) / 2.0


def lower_table():
    z = nodes()
    child = -0.25 + z / 2.0
    table = np.ones((P_SIZE, P_SIZE))
    for m in range(P_SIZE):
        for j in range(P_SIZE):
            if j != m:
                table[m] *= (child - z[j]) / (z[m] - z[j])
    return table


Z = [float(v) for v in nodes()]
LOW = lower_table()
POINTS = [((f + 0.5) / EV - 0.5, ((3 * f) % EV + 0.5) / EV - 0.5) for f in range(EV)]


def turn(theta):
    u = theta - jnp.round(theta)
    w = u * u
    s = SIN[4]
    c = COS[4]
    for k in (3, 2, 1, 0):
        s = s * w + SIN[k]
        c = c * w + COS[k]
    s = s * u
    return 1.0 - s * s, s * c


def interpolate(low, high):
    even = [low[j] + high[4 - j] for j in range(5)]
    odd = [low[j] - high[4 - j] for j in range(5)]
    out = [None] * 5
    for m in (0, 1):
        a = sum_of(even, [0.5 * (LOW[m, j] + LOW[4 - m, j]) for j in range(5)])
        b = sum_of(odd, [0.5 * (LOW[m, j] - LOW[4 - m, j]) for j in range(5)])
        out[m] = a + b
        out[4 - m] = a - b
    out[2] = sum_of(even, [LOW[2, j] for j in range(5)])
    return out


def sum_of(values, factors):
    total = None
    for v, f in zip(values, factors):
        if abs(f) < 1e-14:
            continue
        term = v * float(f)
        total = term if total is None else total + term
    return total


def speeds(x1, x2):
    cp, _ = turn(x1 - x2)
    cq, _ = turn(x1 + x2)
    return (2.0 + 0.5 * (cp - cq)) * 0.0625, (2.0 + 0.5 * (cp + cq)) * 0.0625


def moved(x1, x2, c1, c2, d1, d2):
    dp, dq = d1 - d2, d1 + d2
    _, sp = turn(x1 - x2 + 0.5 * dp)
    _, sq = turn(x1 + x2 + 0.5 * dq)
    gp = sp * (-2.0 * math.sin(math.pi * dp))
    gq = sq * (-2.0 * math.sin(math.pi * dq))
    e1 = (gp - gq) * 0.03125
    e2 = (gp + gq) * 0.03125
    n1, n2 = c1 + e1, c2 + e2
    return n1 * n1, n2 * n2, e1 * (c1 + n1), e2 * (c2 + n2)


def root(s):
    return s * lax.rsqrt(s)


def inverse(s):
    return pltpu.reciprocal(s, approx=True)


def kernel(w_ref, o_ref, send, recv, st0, st1, tab, nrm, acc, part, final, send_sem, recv_sem, own_sem, fs_sem, fr_sem):
    bx, by = lax.axis_index("bx"), lax.axis_index("by")
    gi, gj = bx // 4, by // 4
    b0, b1 = bx % 2, (bx // 2) % 2
    c0, c1 = by % 2, (by // 2) % 2
    me = b0 + 2 * c0 + 4 * b1 + 8 * c1
    slot = gi * 4 + gj
    s_b1, s_c1, s_c0, s_b0 = gi // 4, (gi // 2) % 2, gi % 2, gj // 2
    source_x, source_y = s_b0 + 2 * s_b1, s_c0 + 2 * s_c1
    my_line, my_half = gj // 2, gj % 2
    is_self = (b0 == s_b0) & (b1 == s_b1) & (c0 == s_c0) & (c1 == s_c1)

    def peer(k):
        flip = lambda bit, at: (1 - bit) if (k >> at) & 1 else bit
        q0, r0, q1, r1 = flip(b0, 0), flip(c0, 1), flip(b1, 2), flip(c1, 3)
        return q0 + 2 * r0 + 4 * q1 + 8 * r1, (gi * 4 + q0 + 2 * q1, gj * 4 + r0 + 2 * r1)

    order = [k for k in range(16) if k & 2] + [k for k in range(1, 16) if not k & 2]

    barrier = pltpu.get_barrier_semaphore()
    for k in order:
        pl.semaphore_signal(barrier, inc=1, device_id=peer(k)[1], device_id_type=MESH)

    @pl.loop(0, 32)
    def _(g):
        @pl.when(jnp.logical_not(is_self & (g == slot)))
        def _():
            pl.semaphore_signal(
                barrier,
                inc=1,
                device_id=((g // 4) * 4 + source_x, (g % 4) * 4 + source_y),
                device_id_type=MESH,
            )

    lane = lax.broadcasted_iota(jnp.int32, (8, 128), 1)
    sub = lax.broadcasted_iota(jnp.int32, (8, 128), 0)
    bit = lambda v, at: (v >> at) & 1
    l6, l5, l4, l3 = (bit(lane, at) for at in (6, 5, 4, 3))
    s2, s1, s0 = (bit(sub, at) for at in (2, 1, 0))

    def shuffle(r):
        half, row = r // ROWS, r % ROWS
        x = [w_ref[row, 2 * half + q] for q in range(2)]
        y = [
            jnp.where(l5 == 0, x[0], pltpu.roll(x[1], 32, 1)),
            jnp.where(l5 == 0, pltpu.roll(x[0], 96, 1), x[1]),
        ]
        for h in range(2):
            v = y[h]
            v = jnp.where(s2 == l6, v, pltpu.roll(pltpu.roll(v, 4, 0), 64, 1))
            for s_bit, l_bit, by_sub, by_lane in ((s1, l4, 2, 16), (s0, l3, 1, 8)):
                up = pltpu.roll(pltpu.roll(v, 8 - by_sub, 0), by_lane, 1)
                down = pltpu.roll(pltpu.roll(v, by_sub, 0), 128 - by_lane, 1)
                v = jnp.where(s_bit == l_bit, v, jnp.where(s_bit == 0, up, down))
            send[pl.ds(h * 8 * SLOT + r, 8, stride=SLOT), :] = v

    def exchange(half, k):
        at, device = peer(k)
        start, count = ((0, FIRST), (FIRST, SLOT - FIRST))[half]
        return pltpu.make_async_remote_copy(
            src_ref=send.at[pl.ds(pl.multiple_of(at * SLOT + start, 8), count)],
            dst_ref=recv.at[pl.ds(pl.multiple_of(me * SLOT + start, 8), count)],
            send_sem=send_sem.at[half, k],
            recv_sem=recv_sem.at[half, k],
            device_id=device,
            device_id_type=MESH,
        )

    def own(half):
        start, count = ((0, FIRST), (FIRST, SLOT - FIRST))[half]
        rows = pl.ds(pl.multiple_of(me * SLOT + start, 8), count)
        return pltpu.make_async_copy(send.at[rows], recv.at[rows], own_sem.at[half])

    @pl.loop(0, FIRST // 4)
    def _(g):
        for u in range(4):
            shuffle(g * 4 + u)

    pl.semaphore_wait(barrier, 47 - is_self.astype(jnp.int32))
    for k in order:
        exchange(0, k).start()
    own(0).start()

    @pl.loop(FIRST // 4, NODES)
    def _(g):
        for u in range(4):
            shuffle(g * 4 + u)

    for k in order:
        exchange(1, k).start()
    own(1).start()

    f32 = lambda v: v.astype(jnp.float32)
    q_bit = l5
    box2 = 4 * l6 + 2 * l4 + l3
    line1 = 4 * b1 + 2 * c1 + c0
    line2 = 8 * b0 + (lane & 7)
    xa1 = (f32(jnp.zeros_like(lane) + ((17 * line1 + 3) % 128)) + 0.5) * (1.0 / 128)
    xa2 = (f32((29 * line2 + 11) & 127) + 0.5) * (1.0 / 128)
    m2, m1, m0 = f32(s2), f32(s1), f32(s0)
    h1, h2 = 1.0 / 256, 1.0 / 512

    def center(index, width):
        return f32(index) * width + (0.5 * width - N / 2.0)

    def split(level, p, load, dst):
        first = level == 0
        along = level % 2
        box1 = 2 * p + q_bit
        if level == 0:
            index = [lambda c: box1 * 32 + 4 * gi + 2 * s1 + c, lambda c: box2 * 16 + 4 * gj + 2 * s2 + s0]
            widths, x, step = (128.0, 128.0), (xa1, xa2), h1
        elif level == 1:
            index = [lambda c: box1 * 16 + 2 * gi + s0, lambda c: box2 * 16 + 4 * gj + 2 * s1 + c]
            widths, x, step = (256.0, 128.0), (xa1 + (m2 - 0.5) * h1, xa2), h1
        elif level == 2:
            index = [lambda c: box1 * 16 + 2 * gi + c, lambda c: box2 * 8 + 2 * gj + s0]
            widths, x, step = (256.0, 256.0), (xa1 + (m1 - 0.5) * h1, xa2 + (m2 - 0.5) * h1), h2
        else:
            index = [lambda c: box1 * 8 + gi, lambda c: box2 * 8 + 2 * gj + c]
            widths = (512.0, 256.0)
            x, step = (xa1 + (m0 - 0.5) * h1 + (m2 - 0.5) * h2, xa2 + (m1 - 0.5) * h1), h2
        speed = speeds(*x)
        base = (speed[0] * speed[0], speed[1] * speed[1])
        steps = ((e - 0.5) * step for e in range(2))
        new = []
        for s in steps:
            shift = (s, 0.0) if along == 0 else (0.0, s)
            new.append(moved(x[0], x[1], speed[0], speed[1], *shift) + (s,))
        other = 1 - along
        corner = []
        for c in range(2):
            mid = center(index[along](c), widths[along])
            for i in range(5):
                off = widths[along] * Z[i]
                k = mid + off
                sq = k * k
                if not first:
                    tab[0, c * 5 + i] = base[along] * sq
                for e in range(2):
                    a = new[e]
                    diff = a[2 + along] * sq
                    line = a[4] * k
                    if first:
                        diff += base[along] * (off * (k + mid))
                        line = a[4] * mid + (x[along] + a[4]) * off
                    tab[1 + 3 * e, c * 5 + i] = a[along] * sq
                    tab[2 + 3 * e, c * 5 + i] = diff
                    tab[3 + 3 * e, c * 5 + i] = line
            corner.append(base[along] * (mid * mid))
        mid = center(index[other](0), widths[other])
        for i in range(5):
            off = widths[other] * Z[i]
            k = mid + off
            sq = k * k
            tab[0, 10 + i] = x[other] * off if first else base[other] * sq
            for e in range(2):
                diff = new[e][2 + other] * sq
                if first:
                    diff += base[other] * (off * (k + mid))
                tab[1 + 3 * e, 10 + i] = new[e][other] * sq
                tab[2 + 3 * e, 10 + i] = diff
        if first:
            for c in range(2):
                nrm[c] = root(corner[c] + base[other] * (mid * mid))

        @pl.loop(0, 5)
        def _(j):
            point = lambda i: (i * 5 + j) if along == 0 else (j * 5 + i)
            shared = tab[0, 10 + j]
            norms = []
            if not first:
                for c in range(2):
                    norms.append([root(tab[0, c * 5 + i] + shared) for i in range(5)])
            for e in range(2):
                norm_o, diff_o = tab[1 + 3 * e, 10 + j], tab[2 + 3 * e, 10 + j]
                real, imag = [], []
                for c in range(2):
                    rr, ii = [], []
                    for i in range(5):
                        at = c * 5 + i
                        old = nrm[c] if first else norms[c][i]
                        theta = tab[3 + 3 * e, at] + (tab[2 + 3 * e, at] + diff_o) * inverse(
                            root(tab[1 + 3 * e, at] + norm_o) + old
                        )
                        if first:
                            theta = theta + shared
                        cs, sn = turn(theta)
                        vr, vi = load(c, 0, point(i)), load(c, 1, point(i))
                        rr.append(vr * cs - vi * sn)
                        ii.append(vr * sn + vi * cs)
                    real.append(rr)
                    imag.append(ii)
                for comp, terms in ((0, real), (1, imag)):
                    out = interpolate(terms[0], terms[1])
                    for i in range(5):
                        dst[comp * NODES + point(i), pl.ds(8 * e, 8), :] = out[i]

    def evaluate(p, src):
        k1 = [center((2 * p + q_bit) * 8 + gi, 512.0) + 512.0 * z for z in Z]
        k2 = [center(box2 * 4 + gj, 512.0) + 512.0 * z for z in Z]
        x1 = xa1 + (m0 - 0.5) * h1 + (m2 - 0.5) * h2
        x2 = [xa2 + (m1 - 0.5) * h1 + (h - 0.5) * h2 for h in range(2)]
        speed = [speeds(x1, x2[h]) for h in range(2)]
        for i in range(5):
            tab[0, i] = k1[i]
            tab[0, 5 + i] = k2[i]
            tab[1, i] = k1[i] * k1[i]
            tab[1, 5 + i] = k2[i] * k2[i]
        for h in range(2):
            t1 = [speed[h][0] * speed[h][0] * (k * k) for k in k1]
            t2 = [speed[h][1] * speed[h][1] * (k * k) for k in k2]
            for i in range(5):
                for j in range(5):
                    nrm[h * NODES + i * 5 + j] = root(t1[i] + t2[j])

        for f in range(EV):
            d1, d2 = h2 * POINTS[f][0], h2 * POINTS[f][1]
            new = [moved(x1, x2[h], speed[h][0], speed[h][1], d1, d2) for h in range(2)]
            line1 = [tab[0, i] * d1 for i in range(5)]
            line2 = [tab[0, 5 + i] * d2 for i in range(5)]
            for h in range(2):
                a = new[h]
                n1 = [a[0] * tab[1, i] for i in range(5)]
                n2 = [a[1] * tab[1, 5 + i] for i in range(5)]
                g1 = [a[2] * tab[1, i] for i in range(5)]
                g2 = [a[3] * tab[1, 5 + i] for i in range(5)]
                real, imag = None, None
                for i in range(5):
                    for j in range(5):
                        t = i * 5 + j
                        theta = (line1[i] + line2[j]) + (g1[i] + g2[j]) * inverse(
                            root(n1[i] + n2[j]) + nrm[h * NODES + t]
                        )
                        cs, sn = turn(theta)
                        vr, vi = src[t, pl.ds(8 * h, 8), :], src[NODES + t, pl.ds(8 * h, 8), :]
                        rr = vr * cs - vi * sn
                        ii = vr * sn + vi * cs
                        real = rr if real is None else real + rr
                        imag = ii if imag is None else imag + ii
                acc[2 * f, pl.ds(8 * h, 8), :] += real
                acc[2 * f + 1, pl.ds(8 * h, 8), :] += imag

    acc[...] = jnp.zeros_like(acc)

    def work(p):
        def arrived(c, comp, t):
            return recv[pl.ds(c * SLOT + p * ROWS + comp * NODES + t, 8, stride=2 * SLOT), :]

        def held(src):
            return lambda c, comp, t: src[comp * NODES + t, pl.ds(c, 8, stride=2), :]

        split(0, p, arrived, st0)
        split(1, p, held(st0), st1)
        split(2, p, held(st1), st0)
        split(3, p, held(st0), st1)
        evaluate(p, st1)

    @pl.loop(0, 2)
    def _(p):
        @pl.when(p == 0)
        def _():
            own(0).wait()
            for k in order:
                exchange(0, k).wait()

        @pl.when(p == 1)
        def _():
            own(1).wait()
            for k in order:
                exchange(1, k).wait()

        work(p)

    for h in range(2):
        level = [acc[g, pl.ds(8 * h, 8), :] for g in range(16)]
        for l_bit, by_lane in ((l6, 64), (l5, 32), (l4, 16), (l3, 8)):
            count = len(level) // 2
            merged = []
            for g in range(count):
                u, v = level[g], level[g + count]
                keep = jnp.where(l_bit == 0, u, v)
                give = jnp.where(l_bit == 0, v, u)
                merged.append(
                    keep + jnp.where(l_bit == 0, pltpu.roll(give, 128 - by_lane, 1), pltpu.roll(give, by_lane, 1))
                )
            level = merged
        total = level[0] * (1.0 / (P_SIZE * LEVEL_BOXES))
        for e in range(8):
            part[8 * h + e] = total[e : e + 1, :]

    def hand(e, half):
        e4, e3, e2, e1 = (e >> 3) & 1, (e >> 2) & 1, (e >> 1) & 1, e & 1
        return pltpu.make_async_remote_copy(
            src_ref=part.at[e],
            dst_ref=final.at[slot],
            send_sem=fs_sem.at[e, half],
            recv_sem=fr_sem.at[slot],
            device_id=(4 * line1 + 2 * e3 + e1, 4 * (2 * b0 + half) + 2 * e4 + e2),
            device_id_type=MESH,
        )

    def mine(e, half):
        return is_self & (me == e) & (my_half == half)

    for e in range(16):
        for half in range(2):

            @pl.when(jnp.logical_not(mine(e, half)))
            def _():
                hand(e, half).start()

    @pl.when(is_self)
    def _():
        final[slot] = part[me]

    @pl.loop(0, 32)
    def _(g):
        @pl.when(jnp.logical_not(is_self & (g == slot)))
        def _():
            pltpu.make_async_remote_copy(
                src_ref=part.at[0],
                dst_ref=final.at[g],
                send_sem=fs_sem.at[0, 0],
                recv_sem=fr_sem.at[g],
                device_id=((g // 4) * 4 + source_x, (g % 4) * 4 + source_y),
                device_id_type=MESH,
            ).wait_recv()

    total = final[0]
    for g in range(1, 32):
        total = total + final[g]
    total = jnp.where(my_half == 1, pltpu.roll(total, 124, 1), total)
    for g in range(16):
        row = total if g == 0 else pltpu.roll(total, 128 - 8 * g, 1)
        o_ref[g // 2, g % 2] = row[:, :4]

    for e in range(16):
        for half in range(2):

            @pl.when(jnp.logical_not(mine(e, half)))
            def _():
                hand(e, half).wait_send()


def local(weights):
    vmem = pltpu.VMEM
    dma = pltpu.SemaphoreType.DMA
    return pl.pallas_call(
        kernel,
        out_shape=jax.ShapeDtypeStruct((EV, 2, 1, 4), jnp.float32),
        in_specs=[pl.BlockSpec(memory_space=vmem)],
        out_specs=pl.BlockSpec(memory_space=vmem),
        scratch_shapes=[
            vmem((16 * SLOT, 128), jnp.float32),
            vmem((16 * SLOT, 128), jnp.float32),
            vmem((ROWS, 16, 128), jnp.float32),
            vmem((ROWS, 16, 128), jnp.float32),
            vmem((7, 15, 8, 128), jnp.float32),
            vmem((ROWS, 8, 128), jnp.float32),
            vmem((16, 16, 128), jnp.float32),
            vmem((16, 1, 128), jnp.float32),
            vmem((32, 1, 128), jnp.float32),
            dma((2, 16)),
            dma((2, 16)),
            dma((2,)),
            dma((16, 2)),
            dma((32,)),
        ],
        compiler_params=pltpu.CompilerParams(
            collective_id=0, has_side_effects=True, vmem_limit_bytes=48 * 1024 * 1024
        ),
    )(weights.reshape(ROWS, 4, 8, 128))


def solution(mesh):
    return jax.shard_map(
        local,
        mesh=mesh,
        in_specs=(P(None, None, "bx", "by", None),),
        out_specs=P(None, None, "bx", "by"),
        check_vma=False,
    )
```

```python
import functools
import math

import jax
import jax.numpy as jnp
import numpy as np
from jax import lax
from jax.experimental import pallas as pl
from jax.experimental.pallas import tpu as pltpu
from jax.sharding import PartitionSpec as P

N = 16384
P_SIZE = 5
LEVEL_BOXES = 128
EV = 8
NODES = P_SIZE * P_SIZE
ROWS = 2 * NODES
PHASES = 4
SLOT = 104
PIECES = ((0, 32), (32, 24), (56, 24), (80, 24))
FAR = ((4, 0), (8, 0), (16, 0), (0, 4), (0, 8))
MESH = pl.DeviceIdType.MESH

SIN = (4.44288292, -7.3082457, 3.60635441, -0.84611289, 0.10982699)
COS = (1.4142135, -6.97885099, 5.73946117, -1.88356299, 0.31069819)


def nodes():
    return np.cos(np.pi * (2.0 * np.arange(P_SIZE) + 1.0) / (2.0 * P_SIZE)) / 2.0


def lower_table():
    z = nodes()
    child = -0.25 + z / 2.0
    table = np.ones((P_SIZE, P_SIZE))
    for m in range(P_SIZE):
        for j in range(P_SIZE):
            if j != m:
                table[m] *= (child - z[j]) / (z[m] - z[j])
    return table


Z = [float(v) for v in nodes()]
LOW = lower_table()
POINTS = [((f + 0.5) / EV - 0.5, ((3 * f) % EV + 0.5) / EV - 0.5) for f in range(EV)]


def turn(theta):
    u = theta - jnp.round(theta)
    w = u * u
    s = SIN[4]
    c = COS[4]
    for k in (3, 2, 1, 0):
        s = s * w + SIN[k]
        c = c * w + COS[k]
    s = s * u
    return 1.0 - s * s, s * c


def interpolate(low, high):
    even = [low[j] + high[4 - j] for j in range(5)]
    odd = [low[j] - high[4 - j] for j in range(5)]
    out = [None] * 5
    for m in (0, 1):
        a = sum_of(even, [0.5 * (LOW[m, j] + LOW[4 - m, j]) for j in range(5)])
        b = sum_of(odd, [0.5 * (LOW[m, j] - LOW[4 - m, j]) for j in range(5)])
        out[m] = a + b
        out[4 - m] = a - b
    out[2] = sum_of(even, [LOW[2, j] for j in range(5)])
    return out


def sum_of(values, factors):
    total = None
    for v, f in zip(values, factors):
        if abs(f) < 1e-14:
            continue
        term = v * float(f)
        total = term if total is None else total + term
    return total


def speeds(x1, x2):
    cp, _ = turn(x1 - x2)
    cq, _ = turn(x1 + x2)
    return (2.0 + 0.5 * (cp - cq)) * 0.0625, (2.0 + 0.5 * (cp + cq)) * 0.0625


def moved(x1, x2, c1, c2, d1, d2, sign=None):
    dp, dq = d1 - d2, d1 + d2
    half = 0.5 if sign is None else 0.5 * sign
    _, sp = turn(x1 - x2 + half * dp)
    _, sq = turn(x1 + x2 + half * dq)
    gp = sp * (-2.0 * math.sin(math.pi * dp))
    gq = sq * (-2.0 * math.sin(math.pi * dq))
    e1 = (gp - gq) * 0.03125
    e2 = (gp + gq) * 0.03125
    if sign is not None:
        e1, e2 = e1 * sign, e2 * sign
    n1, n2 = c1 + e1, c2 + e2
    return n1 * n1, n2 * n2, e1 * (c1 + n1), e2 * (c2 + n2)


def root(s):
    return s * lax.rsqrt(s)


def inverse(s):
    return pltpu.reciprocal(s, approx=True)


def kernel(w_hbm, o_ref, w_ref, send, recv, st0, st1, geo, acc, part, final,
           load_sem, send_sem, recv_sem, own_sem, far_sem, fs_sem, fr_sem):
    bx, by = lax.axis_index("bx"), lax.axis_index("by")
    gi, gj = bx // 4, by // 4
    b0, b1 = bx % 2, (bx // 2) % 2
    c0, c1 = by % 2, (by // 2) % 2
    me = b0 + 2 * c0 + 4 * b1 + 8 * c1
    mine_d = (16 - me) % 16
    slot = gi * 4 + gj
    source = (16 - (2 * gi + gj // 2)) % 16
    source_x, source_y = source % 2 + 2 * ((source // 4) % 2), (source // 2) % 2 + 2 * (source // 8)
    my_half = gj % 2
    is_self = source == me

    load = pltpu.make_async_copy(w_hbm, w_ref, load_sem)
    load.start()

    def peer(k):
        flip = lambda bit, at: (1 - bit) if (k >> at) & 1 else bit
        q0, r0, q1, r1 = flip(b0, 0), flip(c0, 1), flip(b1, 2), flip(c1, 3)
        return q0 + 2 * r0 + 4 * q1 + 8 * r1, (gi * 4 + q0 + 2 * q1, gj * 4 + r0 + 2 * r1)

    def far(n):
        def flip(v, size):
            return v + size * (1 - 2 * ((v // size) % 2)) if size else v

        return flip(bx, FAR[n][0]), flip(by, FAR[n][1])

    order = [k for k in range(16) if k & 2] + [k for k in range(1, 16) if not k & 2]

    barrier = pltpu.get_barrier_semaphore()
    for k in order:
        pl.semaphore_signal(barrier, inc=1, device_id=peer(k)[1], device_id_type=MESH)
    for n in range(5):
        pl.semaphore_signal(barrier, inc=1, device_id=far(n), device_id_type=MESH)

    def far_signal(n):
        pl.semaphore_signal(far_sem.at[n], inc=1, device_id=far(n), device_id_type=MESH)

    def far_wait(n):
        pl.semaphore_wait(far_sem.at[n], 1)

    lane = lax.broadcasted_iota(jnp.int32, (8, 128), 1)
    sub = lax.broadcasted_iota(jnp.int32, (8, 128), 0)
    bit = lambda v, at: (v >> at) & 1
    s2, s1, s0 = (bit(sub, at) for at in (2, 1, 0))
    l6, l5, l4, l3 = (bit(lane, at) for at in (6, 5, 4, 3))

    def shuffle(r):
        phase, t = r // NODES, r % NODES
        a = pltpu.roll(w_ref[t, phase], 0, 1, stride=8, stride_axis=0)
        b = pltpu.roll(w_ref[NODES + t, phase], 64, 1, stride=8, stride_axis=0)
        for by_row, l_bit in ((1, l3), (2, l4), (4, l5)):
            ra, rb = pltpu.roll(a, 8 - by_row, 0), pltpu.roll(b, 8 - by_row, 0)
            wraps = sub >= 8 - by_row
            go, wrap = (l_bit == 1) & jnp.logical_not(wraps), (l_bit == 1) & wraps
            a, b = jnp.where(go, ra, jnp.where(wrap, rb, a)), jnp.where(go, rb, jnp.where(wrap, ra, b))
        a, b = jnp.where(l6 == 1, b, a), jnp.where(l6 == 1, a, b)
        send[pl.ds(r, 8, stride=SLOT), :] = a
        send[pl.ds(8 * SLOT + r, 8, stride=SLOT), :] = b

    def exchange(p, k):
        at, device = peer(k)
        start, count = PIECES[p]
        return pltpu.make_async_remote_copy(
            src_ref=send.at[pl.ds(pl.multiple_of(at * SLOT + start, 8), count)],
            dst_ref=recv.at[pl.ds(pl.multiple_of(me * SLOT + start, 8), count)],
            send_sem=send_sem.at[p, k],
            recv_sem=recv_sem.at[p, k],
            device_id=device,
            device_id_type=MESH,
        )

    def own(p):
        start, count = PIECES[p]
        rows = pl.ds(pl.multiple_of(me * SLOT + start, 8), count)
        return pltpu.make_async_copy(send.at[rows], recv.at[rows], own_sem.at[p])

    load.wait()
    for p in range(PHASES):
        start, count = PIECES[p]

        @pl.loop(start // 4, min(start + count, PHASES * NODES) // 4)
        def _(g):
            for u in range(4):
                shuffle(g * 4 + u)

        if p == 0:
            pl.semaphore_wait(barrier, 20)
        for k in order:
            exchange(p, k).start()
        own(p).start()
        if p == 0:
            far_signal(0)

    f32 = lambda v: v.astype(jnp.float32)
    source_row = ((lane >> 3) + (16 - mine_d)) & 15
    box2 = source_row & 7
    last = source_row >> 3
    line1 = mine_d // 2
    line2 = 8 * (mine_d % 2) + (lane & 7)
    xa1 = (f32(jnp.zeros_like(lane) + ((17 * line1 + 3) % 128)) + 0.5) * (1.0 / 128)
    xa2 = (f32((29 * line2 + 11) & 127) + 0.5) * (1.0 / 128)
    m2, m1, m0 = f32(s2) - 0.5, f32(s1) - 0.5, f32(s0) - 0.5
    m3 = f32(last) - 0.5
    h1, h2 = 1.0 / 256, 1.0 / 512
    places = (
        (xa1, xa2),
        (xa1 + m1 * h1, xa2),
        (xa1 + m0 * h1, xa2 + m1 * h1),
        (xa1 + m0 * h1 + m2 * h2, xa2 + m1 * h1),
        (xa1 + m0 * h1 + m2 * h2, xa2 + m1 * h1 + m3 * h2),
    )
    signs = tuple(2.0 * m for m in (m2, m2, m2, m3))
    steps = (0.5 * h1, 0.5 * h1, 0.5 * h2, 0.5 * h2)

    def center(index, width):
        return f32(index) * width + (0.5 * width - N / 2.0)

    def prepare():
        for level in range(4):
            x, d = places[level], steps[level]
            c = speeds(*x)
            shift = (d, 0.0) if level % 2 == 0 else (0.0, d)
            for n, v in enumerate((c[0] * c[0], c[1] * c[1]) + moved(*x, *c, *shift, signs[level])):
                geo[6 * level + n] = v
        x = places[4]
        c = speeds(*x)
        geo[24], geo[25] = c[0] * c[0], c[1] * c[1]
        for f in range(EV):
            for n, v in enumerate(moved(*x, *c, h2 * POINTS[f][0], h2 * POINTS[f][1])):
                geo[26 + 4 * f + n] = v

    def split(level, p, load, store):
        first = level == 0
        along = level % 2
        other = 1 - along
        if level == 0:
            index = [lambda c: p * 32 + 4 * gi + 2 * s1 + c, lambda c: box2 * 16 + 4 * gj + 2 * last + s0]
            widths = (128.0, 128.0)
        elif level == 1:
            index = [lambda c: p * 16 + 2 * gi + s0, lambda c: box2 * 16 + 4 * gj + 2 * last + c]
            widths = (256.0, 128.0)
        elif level == 2:
            index = [lambda c: jnp.zeros_like(lane) + (p * 16 + 2 * gi + c), lambda c: box2 * 8 + 2 * gj + last]
            widths = (256.0, 256.0)
        else:
            index = [lambda c: jnp.zeros_like(lane) + (p * 8 + gi), lambda c: box2 * 8 + 2 * gj + c]
            widths = (512.0, 256.0)
        base = (geo[6 * level], geo[6 * level + 1])
        new = (geo[6 * level + 2], geo[6 * level + 3])
        more = (geo[6 * level + 4], geo[6 * level + 5])
        step = signs[level] * steps[level]
        x = places[level]

        def table(dim, c):
            mid = center(index[dim](c), widths[dim])
            old, norm, diff, line = [], [], [], []
            for i in range(5):
                off = widths[dim] * Z[i]
                k = mid + off
                sq = k * k
                norm.append(new[dim] * sq)
                if first:
                    diff.append(more[dim] * sq + base[dim] * (off * (k + mid)))
                    line.append(step * mid + (x[dim] + step) * off if dim == along else x[dim] * off)
                else:
                    old.append(base[dim] * sq)
                    diff.append(more[dim] * sq)
                    line.append(step * k if dim == along else None)
            if first:
                old = base[dim] * (mid * mid)
            return old, norm, diff, line

        side = table(other, 0)
        main = [table(along, c) for c in range(2)]
        fixed = [root(main[c][0] + side[0]) for c in range(2)] if first else None
        for j in range(5):
            point = lambda i: (i * 5 + j) if along == 0 else (j * 5 + i)
            real, imag = [], []
            for c in range(2):
                rr, ii = [], []
                old, norm, diff, line = main[c]
                for i in range(5):
                    here = fixed[c] if first else root(old[i] + side[0][j])
                    theta = line[i] + (diff[i] + side[2][j]) * inverse(root(norm[i] + side[1][j]) + here)
                    if first:
                        theta = theta + side[3][j]
                    cs, sn = turn(theta)
                    vr, vi = load(c, point(i))
                    rr.append(vr * cs - vi * sn)
                    ii.append(vr * sn + vi * cs)
                real.append(rr)
                imag.append(ii)
            for comp, terms in ((0, real), (1, imag)):
                out = interpolate(terms[0], terms[1])
                for i in range(5):
                    store(comp, point(i), out[i])

    def evaluate(p, src):
        mid1 = center(jnp.zeros_like(lane) + (p * 8 + gi), 512.0)
        mid2 = center(box2 * 4 + gj, 512.0)
        k1 = [mid1 + 512.0 * z for z in Z]
        k2 = [mid2 + 512.0 * z for z in Z]
        sq1 = [k * k for k in k1]
        sq2 = [k * k for k in k2]
        for i in range(5):
            for j in range(5):
                st0[i * 5 + j, pl.ds(0, 8), :] = root(geo[24] * sq1[i] + geo[25] * sq2[j])
        for f in range(EV):
            d1, d2 = h2 * POINTS[f][0], h2 * POINTS[f][1]
            a = [geo[26 + 4 * f + n] for n in range(4)]
            n1, n2 = [a[0] * v for v in sq1], [a[1] * v for v in sq2]
            g1, g2 = [a[2] * v for v in sq1], [a[3] * v for v in sq2]
            line1, line2 = [d1 * k for k in k1], [d2 * k for k in k2]
            real, imag = acc[2 * f], acc[2 * f + 1]
            for i in range(5):
                for j in range(5):
                    t = i * 5 + j
                    theta = (line1[i] + line2[j]) + (g1[i] + g2[j]) * inverse(
                        root(n1[i] + n2[j]) + st0[t, pl.ds(0, 8), :]
                    )
                    cs, sn = turn(theta)
                    vr, vi = src[t, pl.ds(0, 8), :], src[NODES + t, pl.ds(0, 8), :]
                    real = real + (vr * cs - vi * sn)
                    imag = imag + (vr * sn + vi * cs)
            acc[2 * f], acc[2 * f + 1] = real, imag

    def work(p):
        lower = sub < 4

        def arrived(c, t):
            v = recv[pl.ds(c * SLOT + p * NODES + t, 8, stride=2 * SLOT), :]
            turned = pltpu.roll(v, 4, 0)
            u0, u1 = jnp.where(lower, v, turned), jnp.where(lower, turned, v)
            return jnp.where(last == 0, u0, pltpu.roll(u1, 64, 1)), jnp.where(last == 0, pltpu.roll(u0, 64, 1), u1)

        def held(src):
            return lambda c, t: tuple(src[q * NODES + t, pl.ds(c, 8, stride=2), :] for q in range(2))

        def across(src):
            def load(c, t):
                v = [src[q * NODES + t, pl.ds(0, 8), :] for q in range(2)]
                return tuple(jnp.where(last == c, u, pltpu.roll(u, 64, 1)) for u in v)

            return load

        def twice(dst):
            def store(q, t, v):
                dst[q * NODES + t, pl.ds(0, 8), :] = v
                dst[q * NODES + t, pl.ds(8, 8), :] = v

            return store

        def once(dst):
            def store(q, t, v):
                dst[q * NODES + t, pl.ds(0, 8), :] = v

            return store

        split(0, p, arrived, twice(st0))
        split(1, p, held(st0), twice(st1))
        split(2, p, held(st1), once(st0))
        split(3, p, across(st0), once(st1))
        evaluate(p, st1)

    acc[...] = jnp.zeros_like(acc)
    prepare()

    @pl.loop(0, PHASES)
    def _(p):
        for q in range(PHASES):

            @pl.when(p == q)
            def _():
                own(q).wait()
                for k in order:
                    exchange(q, k).wait_recv()
                far_wait(q)
                far_signal(q + 1)

        work(p)

    level = [pltpu.roll(acc[g], (16 - mine_d) * 8, 1) for g in range(16)]
    for l_bit, by_lane in ((l5, 32), (l4, 16), (l3, 8)):
        count = len(level) // 2
        merged = []
        for g in range(count):
            u, v = level[g], level[g + count]
            keep = jnp.where(l_bit == 0, u, v)
            give = jnp.where(l_bit == 0, v, u)
            merged.append(
                keep + jnp.where(l_bit == 0, pltpu.roll(give, 128 - by_lane, 1), pltpu.roll(give, by_lane, 1))
            )
        level = merged
    level = [v * (1.0 / (P_SIZE * LEVEL_BOXES)) for v in level]
    totals = (
        jnp.where(l6 == 0, level[0], pltpu.roll(level[1], 64, 1)),
        jnp.where(l6 == 0, pltpu.roll(level[0], 64, 1), level[1]),
    )
    for h in range(2):
        for e in range(8):
            part[8 * h + e] = totals[h][e : e + 1, :]

    def hand(e, half):
        e4, e3, e2, e1 = (e >> 3) & 1, (e >> 2) & 1, (e >> 1) & 1, e & 1
        return pltpu.make_async_remote_copy(
            src_ref=part.at[e],
            dst_ref=final.at[slot],
            send_sem=fs_sem.at[e, half],
            recv_sem=fr_sem.at[slot],
            device_id=(4 * line1 + 2 * e3 + e1, 4 * (2 * (mine_d % 2) + half) + 2 * e4 + e2),
            device_id_type=MESH,
        )

    def mine(e, half):
        return is_self & (me == e) & (my_half == half)

    far_wait(4)
    for e in range(16):
        for half in range(2):

            @pl.when(jnp.logical_not(mine(e, half)))
            def _():
                hand(e, half).start()

    @pl.when(is_self)
    def _():
        final[slot] = part[me]

    for p in range(PHASES):
        for k in order:
            exchange(p, k).wait_send()

    @pl.loop(0, 32)
    def _(g):
        @pl.when(jnp.logical_not(is_self & (g == slot)))
        def _():
            pltpu.make_async_remote_copy(
                src_ref=part.at[0],
                dst_ref=final.at[g],
                send_sem=fs_sem.at[0, 0],
                recv_sem=fr_sem.at[g],
                device_id=((g // 4) * 4 + source_x, (g % 4) * 4 + source_y),
                device_id_type=MESH,
            ).wait_recv()

    total = final[0]
    for g in range(1, 32):
        total = total + final[g]
    total = jnp.where(my_half == 1, pltpu.roll(total, 124, 1), total)
    for q in range(2):
        for f in range(EV):
            at = 64 * q + 8 * f
            row = total if at == 0 else pltpu.roll(total, 128 - at, 1)
            o_ref[f, q] = row[:, :4]

    for e in range(16):
        for half in range(2):

            @pl.when(jnp.logical_not(mine(e, half)))
            def _():
                hand(e, half).wait_send()


def local(weights):
    vmem = pltpu.VMEM
    dma = pltpu.SemaphoreType.DMA
    return pl.pallas_call(
        kernel,
        out_shape=jax.ShapeDtypeStruct((EV, 2, 1, 4), jnp.float32),
        in_specs=[pl.BlockSpec(memory_space=pl.ANY)],
        out_specs=pl.BlockSpec(memory_space=vmem),
        scratch_shapes=[
            vmem((ROWS, 4, 8, 128), jnp.float32),
            vmem((16 * SLOT, 128), jnp.float32),
            vmem((16 * SLOT, 128), jnp.float32),
            vmem((ROWS, 16, 128), jnp.float32),
            vmem((ROWS, 16, 128), jnp.float32),
            vmem((58, 8, 128), jnp.float32),
            vmem((16, 8, 128), jnp.float32),
            vmem((16, 1, 128), jnp.float32),
            vmem((32, 1, 128), jnp.float32),
            dma(()),
            dma((PHASES, 16)),
            dma((PHASES, 16)),
            dma((PHASES,)),
            pltpu.SemaphoreType.REGULAR((5,)),
            dma((16, 2)),
            dma((32,)),
        ],
        compiler_params=pltpu.CompilerParams(
            collective_id=0, has_side_effects=True, vmem_limit_bytes=60 * 1024 * 1024
        ),
    )(weights.reshape(ROWS, 4, 8, 128))


def solution(mesh):
    return jax.shard_map(
        local,
        mesh=mesh,
        in_specs=(P(None, None, "bx", "by", None),),
        out_specs=P(None, None, "bx", "by"),
        check_vma=False,
    )
```

```python
import functools
import math

import jax
import jax.numpy as jnp
import numpy as np
from jax import lax
from jax.experimental import pallas as pl
from jax.experimental.pallas import tpu as pltpu
from jax.sharding import PartitionSpec as P

N = 16384
P_SIZE = 5
LEVEL_BOXES = 128
EV = 8
NODES = P_SIZE * P_SIZE
ROWS = 2 * NODES
PHASES = 4
WIDE = 2
GAP = 6
SLOT = 112
PIECES = ((0, 32), (32, 24), (56, 32), (88, 24))
PARTS = ((0, 32), (32, 50), (50, 82), (82, 100))
MESH = pl.DeviceIdType.MESH

SIN = (4.44288292, -7.3082457, 3.60635441, -0.84611289, 0.10982699)
COS = (1.4142135, -6.97885099, 5.73946117, -1.88356299, 0.31069819)


def nodes():
    return np.cos(np.pi * (2.0 * np.arange(P_SIZE) + 1.0) / (2.0 * P_SIZE)) / 2.0


def lower_table():
    z = nodes()
    child = -0.25 + z / 2.0
    table = np.ones((P_SIZE, P_SIZE))
    for m in range(P_SIZE):
        for j in range(P_SIZE):
            if j != m:
                table[m] *= (child - z[j]) / (z[m] - z[j])
    return table


Z = [float(v) for v in nodes()]
LOW = lower_table()
POINTS = [((f + 0.5) / EV - 0.5, ((3 * f) % EV + 0.5) / EV - 0.5) for f in range(EV)]


def turn(theta):
    u = theta - jnp.round(theta)
    w = u * u
    s = SIN[4]
    c = COS[4]
    for k in (3, 2, 1, 0):
        s = s * w + SIN[k]
        c = c * w + COS[k]
    s = s * u
    return 1.0 - s * s, s * c


def interpolate_one(values, upper):
    values = [jnp.where(upper == 0, values[j], values[4 - j]) for j in range(5)]
    sign = (1 - 2 * upper).astype(jnp.float32)
    out = [None] * 5
    for m in (0, 1):
        a = sum_of(values, [0.5 * (LOW[m, j] + LOW[4 - m, j]) for j in range(5)])
        b = sum_of(values, [0.5 * (LOW[m, j] - LOW[4 - m, j]) for j in range(5)]) * sign
        out[m] = a + b
        out[4 - m] = a - b
    out[2] = sum_of(values, [LOW[2, j] for j in range(5)])
    return out


def interpolate(low, high):
    even = [low[j] + high[4 - j] for j in range(5)]
    odd = [low[j] - high[4 - j] for j in range(5)]
    out = [None] * 5
    for m in (0, 1):
        a = sum_of(even, [0.5 * (LOW[m, j] + LOW[4 - m, j]) for j in range(5)])
        b = sum_of(odd, [0.5 * (LOW[m, j] - LOW[4 - m, j]) for j in range(5)])
        out[m] = a + b
        out[4 - m] = a - b
    out[2] = sum_of(even, [LOW[2, j] for j in range(5)])
    return out


def sum_of(values, factors):
    total = None
    for v, f in zip(values, factors):
        if abs(f) < 1e-14:
            continue
        term = v * float(f)
        total = term if total is None else total + term
    return total


def speeds(x1, x2):
    cp, _ = turn(x1 - x2)
    cq, _ = turn(x1 + x2)
    return (2.0 + 0.5 * (cp - cq)) * 0.0625, (2.0 + 0.5 * (cp + cq)) * 0.0625


def moved(x1, x2, c1, c2, d1, d2, sign=None):
    dp, dq = d1 - d2, d1 + d2
    half = 0.5 if sign is None else 0.5 * sign
    _, sp = turn(x1 - x2 + half * dp)
    _, sq = turn(x1 + x2 + half * dq)
    gp = sp * (-2.0 * math.sin(math.pi * dp))
    gq = sq * (-2.0 * math.sin(math.pi * dq))
    e1 = (gp - gq) * 0.03125
    e2 = (gp + gq) * 0.03125
    if sign is not None:
        e1, e2 = e1 * sign, e2 * sign
    n1, n2 = c1 + e1, c2 + e2
    return n1 * n1, n2 * n2, e1 * (c1 + n1), e2 * (c2 + n2)


def root(s):
    return s * lax.rsqrt(s)


def inverse(s):
    return pltpu.reciprocal(s, approx=True)


def kernel(w_hbm, o_ref, w_ref, send, recv, st0, st1, st2, st3, norms, geo, lanes, acc, gift_out, gift_in, part, final,
           load_sem, send_sem, recv_sem, own_sem, far_sem, gift_sem, fs_sem, fr_sem):
    bx, by = lax.axis_index("bx"), lax.axis_index("by")
    gi, gj = bx // 4, by // 4
    b0, b1 = bx % 2, (bx // 2) % 2
    c0, c1 = by % 2, (by // 2) % 2
    me = b0 + 2 * c0 + 4 * b1 + 8 * c1
    mine_d = (16 - me) % 16
    slot = gi * 4 + gj
    source = (16 - (2 * gi + gj // 2)) % 16
    source_x, source_y = source % 2 + 2 * ((source // 4) % 2), (source // 2) % 2 + 2 * (source // 8)
    my_half = gj % 2
    is_self = source == me

    load = pltpu.make_async_copy(w_hbm, w_ref, load_sem)
    load.start()

    def peer(k):
        flip = lambda bit, at: (1 - bit) if (k >> at) & 1 else bit
        q0, r0, q1, r1 = flip(b0, 0), flip(c0, 1), flip(b1, 2), flip(c1, 3)
        return q0 + 2 * r0 + 4 * q1 + 8 * r1, (gi * 4 + q0 + 2 * q1, gj * 4 + r0 + 2 * r1)

    def flipped(at_x, at_y):
        def flip(v, bits):
            for size in (1, 2, 4, 8, 16):
                if bits & size:
                    v = v + size * (1 - 2 * ((v // size) % 2))
            return v

        return flip(bx, at_x), flip(by, at_y)

    near = [k for k in (4, 12, 5, 13, 8, 9, 1)]
    order = [k for k in range(16) if k & 2] + near

    steps_y = ((4, 0), (4, 1))
    steps_far = ((8, 0), (16, 0), (0, 4), (0, 12))
    barrier = pltpu.get_barrier_semaphore()
    for device in [peer(k)[1] for k in near] + [flipped(*at) for at in steps_y + steps_far]:
        pl.semaphore_signal(barrier, inc=1, device_id=device, device_id_type=MESH)

    def tell(n, at):
        pl.semaphore_signal(far_sem.at[n], inc=1, device_id=flipped(*at), device_id_type=MESH)

    def told(n):
        pl.semaphore_wait(far_sem.at[n], 1)

    lane = lax.broadcasted_iota(jnp.int32, (8, 128), 1)
    sub = lax.broadcasted_iota(jnp.int32, (8, 128), 0)
    bit = lambda v, at: (v >> at) & 1
    s2, s1, s0 = (bit(sub, at) for at in (2, 1, 0))
    l6, l5, l4, l3 = (bit(lane, at) for at in (6, 5, 4, 3))

    def shuffle(n):
        phase, t = n // NODES, n % NODES
        r = n + GAP * (n // (WIDE * NODES))
        a = pltpu.roll(w_ref[t, phase], 0, 1, stride=8, stride_axis=0)
        b = pltpu.roll(w_ref[NODES + t, phase], 64, 1, stride=8, stride_axis=0)
        for by_row, l_bit in ((1, l3), (2, l4), (4, l5)):
            ra, rb = pltpu.roll(a, 8 - by_row, 0), pltpu.roll(b, 8 - by_row, 0)
            wraps = sub >= 8 - by_row
            go, wrap = (l_bit == 1) & jnp.logical_not(wraps), (l_bit == 1) & wraps
            a, b = jnp.where(go, ra, jnp.where(wrap, rb, a)), jnp.where(go, rb, jnp.where(wrap, ra, b))
        a, b = jnp.where(l6 == 1, b, a), jnp.where(l6 == 1, a, b)
        send[pl.ds(r, 8, stride=SLOT), :] = a
        send[pl.ds(8 * SLOT + r, 8, stride=SLOT), :] = b

    def exchange(p, k):
        start, count = PIECES[p]
        at, device = peer(k)
        place = me
        if p < WIDE:
            device = peer(k & 13)[1]
            place = b0 + (k & 2) + 4 * b1 + 8 * c1
        return pltpu.make_async_remote_copy(
            src_ref=send.at[pl.ds(pl.multiple_of(at * SLOT + start, 8), count)],
            dst_ref=recv.at[pl.ds(pl.multiple_of(place * SLOT + start, 8), count)],
            send_sem=send_sem.at[p, k],
            recv_sem=recv_sem.at[p, k],
            device_id=device,
            device_id_type=MESH,
        )

    def own(p, k):
        start, count = PIECES[p]
        at = peer(k)[0]
        place = b0 + k + 4 * b1 + 8 * c1 if p < WIDE else me
        return pltpu.make_async_copy(
            send.at[pl.ds(pl.multiple_of(at * SLOT + start, 8), count)],
            recv.at[pl.ds(pl.multiple_of(place * SLOT + start, 8), count)],
            own_sem.at[p, k // 2],
        )

    wide_order = [k | more for k in near for more in (0, 2)]
    orders = [wide_order if p < WIDE else order for p in range(PHASES)]
    owns = [(0, 2) if p < WIDE else (0,) for p in range(PHASES)]

    load.wait()
    for p in range(PHASES):
        low, high = PARTS[p]
        unroll = 4 if (high - low) % 4 == 0 else 2

        @pl.loop(0, (high - low) // unroll)
        def _(g):
            for u in range(unroll):
                shuffle(low + g * unroll + u)

        if p == 0:
            pl.semaphore_wait(barrier, 13)
        if p == WIDE:
            told(2)
        for k in orders[p]:
            exchange(p, k).start()
        for k in owns[p]:
            own(p, k).start()
        if p == 0:
            tell(0, steps_y[0])
            tell(1, steps_y[1])
        if p == 1:
            told(0)
            told(1)
            tell(2, steps_y[1])
        if p == 2:
            tell(3, steps_far[0])

    f32 = lambda v: v.astype(jnp.float32)
    m2, m1, m0 = f32(s2) - 0.5, f32(s1) - 0.5, f32(s0) - 0.5
    h1, h2 = 1.0 / 256, 1.0 / 512
    steps = (0.5 * h1, 0.5 * h1, 0.5 * h2, 0.5 * h2)
    other_d = (16 - peer(2)[0]) % 16

    def lines(d):
        d = jnp.zeros_like(lane) + d
        source_row = ((lane >> 3) + (16 - d)) & 15
        line2 = 8 * (d & 1) + (lane & 7)
        xa1 = (f32((17 * (d >> 1) + 3) & 127) + 0.5) * (1.0 / 128)
        xa2 = (f32((29 * line2 + 11) & 127) + 0.5) * (1.0 / 128)
        return source_row & 7, source_row >> 3, xa1, xa2

    def center(index, width):
        return f32(index) * width + (0.5 * width - N / 2.0)

    def prepare(which, d, levels):
        box2, last, xa1, xa2 = lines(d)
        lanes[which, 0], lanes[which, 1] = box2, last
        m3 = f32(last) - 0.5
        places = (
            (xa1, xa2),
            (xa1 + m1 * h1, xa2),
            (xa1 + m0 * h1, xa2 + m1 * h1),
            (xa1 + m0 * h1 + m2 * h2, xa2 + m1 * h1),
            (xa1 + m0 * h1 + m2 * h2, xa2 + m1 * h1 + m3 * h2),
        )
        for level in levels:
            x, d = places[level], steps[level] if level < 4 else None
            c = speeds(*x)
            if level < 4:
                shift = (d, 0.0) if level % 2 == 0 else (0.0, d)
                sign = 2.0 * (m2 if level < 3 else m3)
                for n, v in enumerate((c[0] * c[0], c[1] * c[1]) + moved(*x, *c, *shift, sign)):
                    geo[which, 6 * level + n] = v
            else:
                geo[which, 24], geo[which, 25] = c[0] * c[0], c[1] * c[1]
                for f in range(EV):
                    for n, v in enumerate(moved(*x, *c, h2 * POINTS[f][0], h2 * POINTS[f][1])):
                        geo[which, 26 + 4 * f + n] = v

    def split(level, p, which, load, store, wide=False):
        box2, last = lanes[which, 0], lanes[which, 1]
        single = wide and level == 1
        below = c0 if wide else s0
        first = level == 0
        along = level % 2
        other = 1 - along
        if level == 0:
            index = [lambda c: p * 32 + 4 * gi + 2 * s1 + c, lambda c: box2 * 16 + 4 * gj + 2 * last + below]
            widths = (128.0, 128.0)
        elif level == 1:
            index = [lambda c: p * 16 + 2 * gi + s0, lambda c: box2 * 16 + 4 * gj + 2 * last + c]
            widths = (256.0, 128.0)
        elif level == 2:
            index = [lambda c: jnp.zeros_like(lane) + (p * 16 + 2 * gi + c), lambda c: box2 * 8 + 2 * gj + last]
            widths = (256.0, 256.0)
        else:
            index = [lambda c: jnp.zeros_like(lane) + (p * 8 + gi), lambda c: box2 * 8 + 2 * gj + c]
            widths = (512.0, 256.0)
        base, new, more = ((geo[which, 6 * level + n], geo[which, 6 * level + n + 1]) for n in (0, 2, 4))
        step = (2.0 * steps[level]) * (m2 if level < 3 else f32(last) - 0.5)
        x = lines(group(which))[2:] if first else None

        def table(dim, c):
            mid = center(index[dim](c), widths[dim])
            old, norm, diff, line = [], [], [], []
            for i in range(5):
                off = widths[dim] * Z[i]
                k = mid + off
                sq = k * k
                norm.append(new[dim] * sq)
                if first:
                    diff.append(more[dim] * sq + base[dim] * (off * (k + mid)))
                    line.append(step * mid + (x[dim] + step) * off if dim == along else x[dim] * off)
                else:
                    old.append(base[dim] * sq)
                    diff.append(more[dim] * sq)
                    line.append(step * k if dim == along else None)
            if first:
                old = base[dim] * (mid * mid)
            return old, norm, diff, line

        side = table(other, 0)
        children = (c0,) if single else (0, 1)
        main = [table(along, c) for c in children]
        fixed = [root(old + side[0]) for old, _, _, _ in main] if first else None
        for j in range(5):
            point = lambda i: (i * 5 + j) if along == 0 else (j * 5 + i)
            real, imag = [], []
            for c in range(len(children)):
                rr, ii = [], []
                old, norm, diff, line = main[c]
                for i in range(5):
                    here = fixed[c] if first else root(old[i] + side[0][j])
                    theta = line[i] + (diff[i] + side[2][j]) * inverse(root(norm[i] + side[1][j]) + here)
                    if first:
                        theta = theta + side[3][j]
                    cs, sn = turn(theta)
                    vr, vi = load(c, point(i))
                    rr.append(vr * cs - vi * sn)
                    ii.append(vr * sn + vi * cs)
                real.append(rr)
                imag.append(ii)
            for comp, terms in ((0, real), (1, imag)):
                out = interpolate_one(terms[0], c0) if single else interpolate(terms[0], terms[1])
                for i in range(5):
                    store(comp, point(i), out[i])

    def evaluate(p, which, src):
        box2 = lanes[which, 0]
        mid1 = center(jnp.zeros_like(lane) + (p * 8 + gi), 512.0)
        mid2 = center(box2 * 4 + gj, 512.0)
        k1 = [mid1 + 512.0 * z for z in Z]
        k2 = [mid2 + 512.0 * z for z in Z]
        sq1 = [k * k for k in k1]
        sq2 = [k * k for k in k2]
        for i in range(5):
            for j in range(5):
                norms[i * 5 + j] = root(geo[which, 24] * sq1[i] + geo[which, 25] * sq2[j])
        for f in range(EV):
            d1, d2 = h2 * POINTS[f][0], h2 * POINTS[f][1]
            a = [geo[which, 26 + 4 * f + n] for n in range(4)]
            n1, n2 = [a[0] * v for v in sq1], [a[1] * v for v in sq2]
            g1, g2 = [a[2] * v for v in sq1], [a[3] * v for v in sq2]
            line1, line2 = [d1 * k for k in k1], [d2 * k for k in k2]
            real, imag = acc[which, 2 * f], acc[which, 2 * f + 1]
            for i in range(5):
                for j in range(5):
                    t = i * 5 + j
                    theta = (line1[i] + line2[j]) + (g1[i] + g2[j]) * inverse(
                        root(n1[i] + n2[j]) + norms[t]
                    )
                    cs, sn = turn(theta)
                    vr, vi = src[t], src[NODES + t]
                    real = real + (vr * cs - vi * sn)
                    imag = imag + (vr * sn + vi * cs)
            acc[which, 2 * f], acc[which, 2 * f + 1] = real, imag

    def group(which):
        if which == 2:
            return jnp.where(s0 == 0, mine_d, other_d)
        return mine_d

    def arrived(p, which, gap):
        last = lanes[which, 1]
        lower = sub < 4

        def load(c, t):
            v = recv[pl.ds(c * SLOT + gap + p * NODES + t, 8, stride=2 * SLOT), :]
            turned = pltpu.roll(v, 4, 0)
            u0, u1 = jnp.where(lower, v, turned), jnp.where(lower, turned, v)
            return jnp.where(last == 0, u0, pltpu.roll(u1, 64, 1)), jnp.where(last == 0, pltpu.roll(u0, 64, 1), u1)

        return load

    def twice(dst):
        def store(q, t, v):
            dst[q * NODES + t, pl.ds(0, 8), :] = v
            dst[q * NODES + t, pl.ds(8, 8), :] = v

        return store

    def once(dst):
        def store(q, t, v):
            dst[q * NODES + t] = v

        return store

    def rest(p, which):
        last = lanes[which, 1]

        def held(c, t):
            return tuple(st1[q * NODES + t, pl.ds(c, 8, stride=2), :] for q in range(2))

        def across(c, t):
            v = [st2[q * NODES + t] for q in range(2)]
            return tuple(jnp.where(last == c, u, pltpu.roll(u, 64, 1)) for u in v)

        split(2, p, which, held, once(st2))
        split(3, p, which, across, once(st3))
        evaluate(p, which, st3)

    def fold(which, d):
        level = [pltpu.roll(acc[which, g], (16 - d) * 8, 1) for g in range(16)]
        for l_bit, by_lane in ((l5, 32), (l4, 16), (l3, 8)):
            count = len(level) // 2
            merged = []
            for g in range(count):
                u, v = level[g], level[g + count]
                keep = jnp.where(l_bit == 0, u, v)
                give = jnp.where(l_bit == 0, v, u)
                merged.append(
                    keep + jnp.where(l_bit == 0, pltpu.roll(give, 128 - by_lane, 1), pltpu.roll(give, by_lane, 1))
                )
            level = merged
        level = [v * (1.0 / (P_SIZE * LEVEL_BOXES)) for v in level]
        return (
            jnp.where(l6 == 0, level[0], pltpu.roll(level[1], 64, 1)),
            jnp.where(l6 == 0, pltpu.roll(level[0], 64, 1), level[1]),
        )

    acc[...] = jnp.zeros_like(acc)
    prepare(2, group(2), (0,))
    prepare(0, mine_d, range(5))
    prepare(1, other_d, range(1, 5))

    def await_piece(q):
        for k in owns[q]:
            own(q, k).wait()
        for k in orders[q]:
            exchange(q, k).wait_recv()

    @pl.loop(0, WIDE)
    def _(p):
        for q in range(WIDE):

            @pl.when(p == q)
            def _():
                await_piece(q)
                told(3 + q)
                tell(4 + q, steps_far[1 + q])

        split(0, p, 2, arrived(p, 2, 0), twice(st0), wide=True)

        @pl.loop(0, 2)
        def _(which):
            def side(c, t):
                return tuple(st0[q * NODES + t, pl.ds(which, 8, stride=2), :] for q in range(2))

            split(1, p, which, side, twice(st1), wide=True)
            rest(p, which)

    gift = pltpu.make_async_remote_copy(
        src_ref=gift_out,
        dst_ref=gift_in,
        send_sem=gift_sem.at[0],
        recv_sem=gift_sem.at[1],
        device_id=flipped(0, 1),
        device_id_type=MESH,
    )
    gift_out[0], gift_out[1] = fold(1, other_d)
    gift.start()

    @pl.loop(WIDE, PHASES)
    def _(p):
        for q in range(WIDE, PHASES):

            @pl.when(p == q)
            def _():
                await_piece(q)
                told(3 + q)
                if q == WIDE:
                    tell(4 + q, steps_far[1 + q])

        def held(c, t):
            return tuple(st0[q * NODES + t, pl.ds(c, 8, stride=2), :] for q in range(2))

        split(0, p, 0, arrived(p, 0, GAP), twice(st0))
        split(1, p, 0, held, twice(st1))
        rest(p, 0)

    gift.wait()
    totals = fold(0, mine_d)
    for h in range(2):
        total = totals[h] + gift_in[h]
        for e in range(8):
            part[8 * h + e] = total[e : e + 1, :]

    line1 = mine_d // 2

    def hand(e, half):
        e4, e3, e2, e1 = (e >> 3) & 1, (e >> 2) & 1, (e >> 1) & 1, e & 1
        return pltpu.make_async_remote_copy(
            src_ref=part.at[e],
            dst_ref=final.at[slot],
            send_sem=fs_sem.at[e, half],
            recv_sem=fr_sem.at[slot],
            device_id=(4 * line1 + 2 * e3 + e1, 4 * (2 * (mine_d % 2) + half) + 2 * e4 + e2),
            device_id_type=MESH,
        )

    def mine(e, half):
        return is_self & (me == e) & (my_half == half)

    for e in range(16):
        for half in range(2):

            @pl.when(jnp.logical_not(mine(e, half)))
            def _():
                hand(e, half).start()

    @pl.when(is_self)
    def _():
        final[slot] = part[me]

    for p in range(PHASES):
        for k in orders[p]:
            exchange(p, k).wait_send()

    @pl.loop(0, 32)
    def _(g):
        @pl.when(jnp.logical_not(is_self & (g == slot)))
        def _():
            pltpu.make_async_remote_copy(
                src_ref=part.at[0],
                dst_ref=final.at[g],
                send_sem=fs_sem.at[0, 0],
                recv_sem=fr_sem.at[g],
                device_id=((g // 4) * 4 + source_x, (g % 4) * 4 + source_y),
                device_id_type=MESH,
            ).wait_recv()

    total = final[0]
    for g in range(1, 32):
        total = total + final[g]
    total = jnp.where(my_half == 1, pltpu.roll(total, 124, 1), total)
    spread = jnp.where((lane & 7) == sub, jnp.broadcast_to(total, (8, 128)), 0.0)
    place = lax.broadcasted_iota(jnp.int32, (128, 128), 0) >> 3
    column = lax.broadcasted_iota(jnp.int32, (128, 128), 1)
    picked = jnp.dot(
        spread,
        jnp.where(place == column, 1.0, 0.0),
        precision=lax.Precision.HIGHEST,
        preferred_element_type=jnp.float32,
    )
    o_ref[0, 0] = picked[:4, :EV]
    o_ref[1, 0] = picked[:4, EV : 2 * EV]

    for e in range(16):
        for half in range(2):

            @pl.when(jnp.logical_not(mine(e, half)))
            def _():
                hand(e, half).wait_send()


def local(weights):
    vmem = pltpu.VMEM
    dma = pltpu.SemaphoreType.DMA
    out = pl.pallas_call(
        kernel,
        out_shape=jax.ShapeDtypeStruct((2, 1, 4, EV), jnp.float32),
        in_specs=[pl.BlockSpec(memory_space=pl.ANY)],
        out_specs=pl.BlockSpec(memory_space=vmem),
        scratch_shapes=[
            vmem((ROWS, 4, 8, 128), jnp.float32),
            vmem((16 * SLOT, 128), jnp.float32),
            vmem((16 * SLOT, 128), jnp.float32),
            vmem((ROWS, 16, 128), jnp.float32),
            vmem((ROWS, 16, 128), jnp.float32),
            vmem((ROWS, 8, 128), jnp.float32),
            vmem((ROWS, 8, 128), jnp.float32),
            vmem((NODES, 8, 128), jnp.float32),
            vmem((3, 58, 8, 128), jnp.float32),
            vmem((3, 2, 8, 128), jnp.int32),
            vmem((2, 16, 8, 128), jnp.float32),
            vmem((2, 8, 128), jnp.float32),
            vmem((2, 8, 128), jnp.float32),
            vmem((16, 1, 128), jnp.float32),
            vmem((32, 1, 128), jnp.float32),
            dma(()),
            dma((PHASES, 16)),
            dma((PHASES, 16)),
            dma((PHASES, 2)),
            pltpu.SemaphoreType.REGULAR((7,)),
            dma((2,)),
            dma((16, 2)),
            dma((32,)),
        ],
        compiler_params=pltpu.CompilerParams(
            collective_id=0, has_side_effects=True, vmem_limit_bytes=60 * 1024 * 1024
        ),
    )(weights.reshape(ROWS, 4, 8, 128))
    return jnp.transpose(out, (3, 0, 1, 2))


def solution(mesh):
    return jax.shard_map(
        local,
        mesh=mesh,
        in_specs=(P(None, None, "bx", "by", None),),
        out_specs=P(None, None, "bx", "by"),
        check_vma=False,
    )
```

```python
import functools
import math

import jax
import jax.numpy as jnp
import numpy as np
from jax import lax
from jax.experimental import pallas as pl
from jax.experimental.pallas import tpu as pltpu
from jax.sharding import PartitionSpec as P

N = 16384
P_SIZE = 5
LEVEL_BOXES = 128
EV = 8
NODES = P_SIZE * P_SIZE
ROWS = 2 * NODES
PHASES = 4
WIDE = 2
STRIDE = 32
SLOT = PHASES * STRIDE
MESH = pl.DeviceIdType.MESH

SIN = (4.44288292, -7.3082457, 3.60635441, -0.84611289, 0.10982699)
COS = (1.4142135, -6.97885099, 5.73946117, -1.88356299, 0.31069819)


def nodes():
    return np.cos(np.pi * (2.0 * np.arange(P_SIZE) + 1.0) / (2.0 * P_SIZE)) / 2.0


def lower_table():
    z = nodes()
    child = -0.25 + z / 2.0
    table = np.ones((P_SIZE, P_SIZE))
    for m in range(P_SIZE):
        for j in range(P_SIZE):
            if j != m:
                table[m] *= (child - z[j]) / (z[m] - z[j])
    return table


Z = [float(v) for v in nodes()]
LOW = lower_table()
POINTS = [((f + 0.5) / EV - 0.5, ((3 * f) % EV + 0.5) / EV - 0.5) for f in range(EV)]


def turn(theta):
    u = theta - jnp.round(theta)
    w = u * u
    s = SIN[4]
    c = COS[4]
    for k in (3, 2, 1, 0):
        s = s * w + SIN[k]
        c = c * w + COS[k]
    s = s * u
    return 1.0 - s * s, s * c


def interpolate_one(values, upper):
    values = [jnp.where(upper == 0, values[j], values[4 - j]) for j in range(5)]
    sign = (1 - 2 * upper).astype(jnp.float32)
    out = [None] * 5
    for m in (0, 1):
        a = sum_of(values, [0.5 * (LOW[m, j] + LOW[4 - m, j]) for j in range(5)])
        b = sum_of(values, [0.5 * (LOW[m, j] - LOW[4 - m, j]) for j in range(5)]) * sign
        out[m] = a + b
        out[4 - m] = a - b
    out[2] = sum_of(values, [LOW[2, j] for j in range(5)])
    return out


def interpolate(low, high):
    even = [low[j] + high[4 - j] for j in range(5)]
    odd = [low[j] - high[4 - j] for j in range(5)]
    out = [None] * 5
    for m in (0, 1):
        a = sum_of(even, [0.5 * (LOW[m, j] + LOW[4 - m, j]) for j in range(5)])
        b = sum_of(odd, [0.5 * (LOW[m, j] - LOW[4 - m, j]) for j in range(5)])
        out[m] = a + b
        out[4 - m] = a - b
    out[2] = sum_of(even, [LOW[2, j] for j in range(5)])
    return out


def sum_of(values, factors):
    total = None
    for v, f in zip(values, factors):
        if abs(f) < 1e-14:
            continue
        term = v * float(f)
        total = term if total is None else total + term
    return total


def speeds(x1, x2):
    cp, _ = turn(x1 - x2)
    cq, _ = turn(x1 + x2)
    return (2.0 + 0.5 * (cp - cq)) * 0.0625, (2.0 + 0.5 * (cp + cq)) * 0.0625


def moved(x1, x2, c1, c2, d1, d2, sign=None):
    dp, dq = d1 - d2, d1 + d2
    half = 0.5 if sign is None else 0.5 * sign
    _, sp = turn(x1 - x2 + half * dp)
    _, sq = turn(x1 + x2 + half * dq)
    gp = sp * (-2.0 * math.sin(math.pi * dp))
    gq = sq * (-2.0 * math.sin(math.pi * dq))
    e1 = (gp - gq) * 0.03125
    e2 = (gp + gq) * 0.03125
    if sign is not None:
        e1, e2 = e1 * sign, e2 * sign
    n1, n2 = c1 + e1, c2 + e2
    return n1 * n1, n2 * n2, e1 * (c1 + n1), e2 * (c2 + n2)


def root(s):
    return s * lax.rsqrt(s)


def inverse(s):
    return pltpu.reciprocal(s, approx=True)


def kernel(w_hbm, o_ref, w_ref, send, recv, st0, st1, st2, st3, norms, geo, lanes, acc, gift_out, gift_in, part, final,
           load_sem, send_sem, recv_sem, own_sem, far_sem, gift_sem, fs_sem, fr_sem):
    bx, by = lax.axis_index("bx"), lax.axis_index("by")
    gi, gj = bx // 4, by // 4
    b0, b1 = bx % 2, (bx // 2) % 2
    c0, c1 = by % 2, (by // 2) % 2
    me = b0 + 2 * c0 + 4 * b1 + 8 * c1
    mine_d = (16 - me) % 16
    slot = gi * 4 + gj
    source = (16 - (2 * gi + gj // 2)) % 16
    source_x, source_y = source % 2 + 2 * ((source // 4) % 2), (source // 2) % 2 + 2 * (source // 8)
    my_half = gj % 2
    is_self = source == me

    load = pltpu.make_async_copy(w_hbm, w_ref, load_sem)
    load.start()

    def peer(k):
        flip = lambda bit, at: (1 - bit) if (k >> at) & 1 else bit
        q0, r0, q1, r1 = flip(b0, 0), flip(c0, 1), flip(b1, 2), flip(c1, 3)
        return q0 + 2 * r0 + 4 * q1 + 8 * r1, (gi * 4 + q0 + 2 * q1, gj * 4 + r0 + 2 * r1)

    def flipped(at_x, at_y):
        def flip(v, bits):
            for size in (1, 2, 4, 8, 16):
                if bits & size:
                    v = v + size * (1 - 2 * ((v // size) % 2))
            return v

        return flip(bx, at_x), flip(by, at_y)

    near = [k for k in (4, 12, 5, 13, 8, 9, 1)]
    order = [k for k in range(16) if k & 2] + near

    steps_y = ((4, 0), (4, 1))
    steps_far = ((8, 0), (16, 0), (0, 4), (0, 12))
    barrier = pltpu.get_barrier_semaphore()
    for device in [peer(k)[1] for k in near] + [flipped(*at) for at in steps_y + steps_far]:
        pl.semaphore_signal(barrier, inc=1, device_id=device, device_id_type=MESH)

    def tell(n, at):
        pl.semaphore_signal(far_sem.at[n], inc=1, device_id=flipped(*at), device_id_type=MESH)

    def told(n):
        pl.semaphore_wait(far_sem.at[n], 1)

    lane = lax.broadcasted_iota(jnp.int32, (8, 128), 1)
    sub = lax.broadcasted_iota(jnp.int32, (8, 128), 0)
    bit = lambda v, at: (v >> at) & 1
    s2, s1, s0 = (bit(sub, at) for at in (2, 1, 0))
    l6, l5, l4, l3 = (bit(lane, at) for at in (6, 5, 4, 3))

    def shuffle(n):
        phase, t = n // NODES, n % NODES
        r = phase * STRIDE + t
        a = pltpu.roll(w_ref[t, phase], 0, 1, stride=8, stride_axis=0)
        b = pltpu.roll(w_ref[NODES + t, phase], 64, 1, stride=8, stride_axis=0)
        for by_row, l_bit in ((1, l3), (2, l4), (4, l5)):
            ra, rb = pltpu.roll(a, 8 - by_row, 0), pltpu.roll(b, 8 - by_row, 0)
            wraps = sub >= 8 - by_row
            go, wrap = (l_bit == 1) & jnp.logical_not(wraps), (l_bit == 1) & wraps
            a, b = jnp.where(go, ra, jnp.where(wrap, rb, a)), jnp.where(go, rb, jnp.where(wrap, ra, b))
        a, b = jnp.where(l6 == 1, b, a), jnp.where(l6 == 1, a, b)
        send[pl.ds(r, 8, stride=SLOT), :] = a
        send[pl.ds(8 * SLOT + r, 8, stride=SLOT), :] = b

    def exchange(p, k):
        start, count = p * STRIDE, NODES
        at, device = peer(k)
        place = me
        if p < WIDE:
            device = peer(k & 13)[1]
            place = b0 + (k & 2) + 4 * b1 + 8 * c1
        return pltpu.make_async_remote_copy(
            src_ref=send.at[pl.ds(pl.multiple_of(at * SLOT + start, 8), count)],
            dst_ref=recv.at[pl.ds(pl.multiple_of(place * SLOT + start, 8), count)],
            send_sem=send_sem.at[p, k],
            recv_sem=recv_sem.at[p, k],
            device_id=device,
            device_id_type=MESH,
        )

    def own(p, k):
        start, count = p * STRIDE, NODES
        at = peer(k)[0]
        place = b0 + k + 4 * b1 + 8 * c1 if p < WIDE else me
        return pltpu.make_async_copy(
            send.at[pl.ds(pl.multiple_of(at * SLOT + start, 8), count)],
            recv.at[pl.ds(pl.multiple_of(place * SLOT + start, 8), count)],
            own_sem.at[p, k // 2],
        )

    wide_order = [k | more for k in near for more in (0, 2)]
    orders = [wide_order if p < WIDE else order for p in range(PHASES)]
    owns = [(0, 2) if p < WIDE else (0,) for p in range(PHASES)]

    def pack(p):
        @pl.loop(0, 5)
        def _(g):
            for u in range(5):
                shuffle(p * NODES + g * 5 + u)

    def ship(p):
        for k in orders[p]:
            exchange(p, k).start()
        for k in owns[p]:
            own(p, k).start()

    load.wait()
    pack(0)
    pl.semaphore_wait(barrier, 13)
    tell(0, steps_y[0])
    tell(1, steps_y[1])
    for p in range(WIDE):
        if p > 0:
            pack(p)
        ship(p)
    told(0)
    told(1)
    tell(2, steps_y[1])
    for p in range(WIDE, PHASES):
        pack(p)
    told(2)
    for p in range(WIDE, PHASES):
        ship(p)
    tell(3, steps_far[0])

    f32 = lambda v: v.astype(jnp.float32)
    m2, m1, m0 = f32(s2) - 0.5, f32(s1) - 0.5, f32(s0) - 0.5
    h1, h2 = 1.0 / 256, 1.0 / 512
    steps = (0.5 * h1, 0.5 * h1, 0.5 * h2, 0.5 * h2)
    other_d = (16 - peer(2)[0]) % 16

    def lines(d):
        d = jnp.zeros_like(lane) + d
        source_row = ((lane >> 3) + (16 - d)) & 15
        line2 = 8 * (d & 1) + (lane & 7)
        xa1 = (f32((17 * (d >> 1) + 3) & 127) + 0.5) * (1.0 / 128)
        xa2 = (f32((29 * line2 + 11) & 127) + 0.5) * (1.0 / 128)
        return source_row & 7, source_row >> 3, xa1, xa2

    def center(index, width):
        return f32(index) * width + (0.5 * width - N / 2.0)

    def prepare(which, d, levels):
        box2, last, xa1, xa2 = lines(d)
        lanes[which, 0], lanes[which, 1] = box2, last
        m3 = f32(last) - 0.5
        places = (
            (xa1, xa2),
            (xa1 + m1 * h1, xa2),
            (xa1 + m0 * h1, xa2 + m1 * h1),
            (xa1 + m0 * h1 + m2 * h2, xa2 + m1 * h1),
            (xa1 + m0 * h1 + m2 * h2, xa2 + m1 * h1 + m3 * h2),
        )
        for level in levels:
            x, d = places[level], steps[level] if level < 4 else None
            c = speeds(*x)
            if level < 4:
                shift = (d, 0.0) if level % 2 == 0 else (0.0, d)
                sign = 2.0 * (m2 if level < 3 else m3)
                for n, v in enumerate((c[0] * c[0], c[1] * c[1]) + moved(*x, *c, *shift, sign)):
                    geo[which, 6 * level + n] = v
            else:
                geo[which, 24], geo[which, 25] = c[0] * c[0], c[1] * c[1]
                for f in range(EV):
                    for n, v in enumerate(moved(*x, *c, h2 * POINTS[f][0], h2 * POINTS[f][1])):
                        geo[which, 26 + 4 * f + n] = v

    def split(level, p, which, load, store, wide=False):
        box2, last = lanes[which, 0], lanes[which, 1]
        single = wide and level == 1
        below = c0 if wide else s0
        first = level == 0
        along = level % 2
        other = 1 - along
        if level == 0:
            index = [lambda c: p * 32 + 4 * gi + 2 * s1 + c, lambda c: box2 * 16 + 4 * gj + 2 * last + below]
            widths = (128.0, 128.0)
        elif level == 1:
            index = [lambda c: p * 16 + 2 * gi + s0, lambda c: box2 * 16 + 4 * gj + 2 * last + c]
            widths = (256.0, 128.0)
        elif level == 2:
            index = [lambda c: jnp.zeros_like(lane) + (p * 16 + 2 * gi + c), lambda c: box2 * 8 + 2 * gj + last]
            widths = (256.0, 256.0)
        else:
            index = [lambda c: jnp.zeros_like(lane) + (p * 8 + gi), lambda c: box2 * 8 + 2 * gj + c]
            widths = (512.0, 256.0)
        base, new, more = ((geo[which, 6 * level + n], geo[which, 6 * level + n + 1]) for n in (0, 2, 4))
        step = (2.0 * steps[level]) * (m2 if level < 3 else f32(last) - 0.5)
        x = lines(group(which))[2:] if first else None

        def table(dim, c):
            mid = center(index[dim](c), widths[dim])
            old, norm, diff, line = [], [], [], []
            for i in range(5):
                off = widths[dim] * Z[i]
                k = mid + off
                sq = k * k
                norm.append(new[dim] * sq)
                if first:
                    diff.append(more[dim] * sq + base[dim] * (off * (k + mid)))
                    line.append(step * mid + (x[dim] + step) * off if dim == along else x[dim] * off)
                else:
                    old.append(base[dim] * sq)
                    diff.append(more[dim] * sq)
                    line.append(step * k if dim == along else None)
            if first:
                old = base[dim] * (mid * mid)
            return old, norm, diff, line

        side = table(other, 0)
        children = (c0,) if single else (0, 1)
        main = [table(along, c) for c in children]
        fixed = [root(old + side[0]) for old, _, _, _ in main] if first else None
        for j in range(5):
            point = lambda i: (i * 5 + j) if along == 0 else (j * 5 + i)
            real, imag = [], []
            for c in range(len(children)):
                rr, ii = [], []
                old, norm, diff, line = main[c]
                for i in range(5):
                    here = fixed[c] if first else root(old[i] + side[0][j])
                    theta = line[i] + (diff[i] + side[2][j]) * inverse(root(norm[i] + side[1][j]) + here)
                    if first:
                        theta = theta + side[3][j]
                    cs, sn = turn(theta)
                    vr, vi = load(c, point(i))
                    rr.append(vr * cs - vi * sn)
                    ii.append(vr * sn + vi * cs)
                real.append(rr)
                imag.append(ii)
            for comp, terms in ((0, real), (1, imag)):
                out = interpolate_one(terms[0], c0) if single else interpolate(terms[0], terms[1])
                for i in range(5):
                    store(comp, point(i), out[i])

    def evaluate(p, which, src):
        box2 = lanes[which, 0]
        mid1 = center(jnp.zeros_like(lane) + (p * 8 + gi), 512.0)
        mid2 = center(box2 * 4 + gj, 512.0)
        k1 = [mid1 + 512.0 * z for z in Z]
        k2 = [mid2 + 512.0 * z for z in Z]
        sq1 = [k * k for k in k1]
        sq2 = [k * k for k in k2]
        for i in range(5):
            for j in range(5):
                norms[i * 5 + j] = root(geo[which, 24] * sq1[i] + geo[which, 25] * sq2[j])
        for f in range(EV):
            d1, d2 = h2 * POINTS[f][0], h2 * POINTS[f][1]
            a = [geo[which, 26 + 4 * f + n] for n in range(4)]
            n1, n2 = [a[0] * v for v in sq1], [a[1] * v for v in sq2]
            g1, g2 = [a[2] * v for v in sq1], [a[3] * v for v in sq2]
            line1, line2 = [d1 * k for k in k1], [d2 * k for k in k2]
            real, imag = acc[which, 2 * f], acc[which, 2 * f + 1]
            for i in range(5):
                for j in range(5):
                    t = i * 5 + j
                    theta = (line1[i] + line2[j]) + (g1[i] + g2[j]) * inverse(
                        root(n1[i] + n2[j]) + norms[t]
                    )
                    cs, sn = turn(theta)
                    vr, vi = src[t], src[NODES + t]
                    real = real + (vr * cs - vi * sn)
                    imag = imag + (vr * sn + vi * cs)
            acc[which, 2 * f], acc[which, 2 * f + 1] = real, imag

    def group(which):
        if which == 2:
            return jnp.where(s0 == 0, mine_d, other_d)
        return mine_d

    def arrived(p, which):
        last = lanes[which, 1]
        lower = sub < 4

        def load(c, t):
            v = recv[pl.ds(c * SLOT + p * STRIDE + t, 8, stride=2 * SLOT), :]
            turned = pltpu.roll(v, 4, 0)
            u0, u1 = jnp.where(lower, v, turned), jnp.where(lower, turned, v)
            return jnp.where(last == 0, u0, pltpu.roll(u1, 64, 1)), jnp.where(last == 0, pltpu.roll(u0, 64, 1), u1)

        return load

    def twice(dst):
        def store(q, t, v):
            dst[q * NODES + t, pl.ds(0, 8), :] = v
            dst[q * NODES + t, pl.ds(8, 8), :] = v

        return store

    def once(dst):
        def store(q, t, v):
            dst[q * NODES + t] = v

        return store

    def rest(p, which):
        last = lanes[which, 1]

        def held(c, t):
            return tuple(st1[q * NODES + t, pl.ds(c, 8, stride=2), :] for q in range(2))

        def across(c, t):
            v = [st2[q * NODES + t] for q in range(2)]
            return tuple(jnp.where(last == c, u, pltpu.roll(u, 64, 1)) for u in v)

        split(2, p, which, held, once(st2))
        split(3, p, which, across, once(st3))
        evaluate(p, which, st3)

    def fold(which, d):
        level = [pltpu.roll(acc[which, g], (16 - d) * 8, 1) for g in range(16)]
        for l_bit, by_lane in ((l5, 32), (l4, 16), (l3, 8)):
            count = len(level) // 2
            merged = []
            for g in range(count):
                u, v = level[g], level[g + count]
                keep = jnp.where(l_bit == 0, u, v)
                give = jnp.where(l_bit == 0, v, u)
                merged.append(
                    keep + jnp.where(l_bit == 0, pltpu.roll(give, 128 - by_lane, 1), pltpu.roll(give, by_lane, 1))
                )
            level = merged
        level = [v * (1.0 / (P_SIZE * LEVEL_BOXES)) for v in level]
        return (
            jnp.where(l6 == 0, level[0], pltpu.roll(level[1], 64, 1)),
            jnp.where(l6 == 0, pltpu.roll(level[0], 64, 1), level[1]),
        )

    acc[...] = jnp.zeros_like(acc)
    prepare(2, group(2), (0,))
    prepare(0, mine_d, range(5))
    prepare(1, other_d, range(1, 5))

    def await_piece(q):
        for k in owns[q]:
            own(q, k).wait()
        for k in orders[q]:
            exchange(q, k).wait_recv()

    @pl.loop(0, WIDE)
    def _(p):
        for q in range(WIDE):

            @pl.when(p == q)
            def _():
                await_piece(q)
                told(3 + q)
                tell(4 + q, steps_far[1 + q])

        split(0, p, 2, arrived(p, 2), twice(st0), wide=True)

        @pl.loop(0, 2)
        def _(which):
            def side(c, t):
                return tuple(st0[q * NODES + t, pl.ds(which, 8, stride=2), :] for q in range(2))

            split(1, p, which, side, twice(st1), wide=True)
            rest(p, which)

    gift = pltpu.make_async_remote_copy(
        src_ref=gift_out,
        dst_ref=gift_in,
        send_sem=gift_sem.at[0],
        recv_sem=gift_sem.at[1],
        device_id=flipped(0, 1),
        device_id_type=MESH,
    )
    gift_out[0], gift_out[1] = fold(1, other_d)
    gift.start()
    told(5)
    tell(6, steps_far[3])

    @pl.loop(WIDE, PHASES)
    def _(p):
        for q in range(WIDE, PHASES):

            @pl.when(p == q)
            def _():
                await_piece(q)

        def held(c, t):
            return tuple(st0[q * NODES + t, pl.ds(c, 8, stride=2), :] for q in range(2))

        split(0, p, 0, arrived(p, 0), twice(st0))
        split(1, p, 0, held, twice(st1))
        rest(p, 0)

    told(6)
    gift.wait()
    totals = fold(0, mine_d)
    for h in range(2):
        total = totals[h] + gift_in[h]
        for e in range(8):
            part[8 * h + e] = total[e : e + 1, :]

    line1 = mine_d // 2

    def hand(e, half):
        e4, e3, e2, e1 = (e >> 3) & 1, (e >> 2) & 1, (e >> 1) & 1, e & 1
        return pltpu.make_async_remote_copy(
            src_ref=part.at[e],
            dst_ref=final.at[slot],
            send_sem=fs_sem.at[e, half],
            recv_sem=fr_sem.at[slot],
            device_id=(4 * line1 + 2 * e3 + e1, 4 * (2 * (mine_d % 2) + half) + 2 * e4 + e2),
            device_id_type=MESH,
        )

    def mine(e, half):
        return is_self & (me == e) & (my_half == half)

    for e in range(16):
        for half in range(2):

            @pl.when(jnp.logical_not(mine(e, half)))
            def _():
                hand(e, half).start()

    @pl.when(is_self)
    def _():
        final[slot] = part[me]

    for p in range(PHASES):
        for k in orders[p]:
            exchange(p, k).wait_send()

    for e in range(16):
        for half in range(2):

            @pl.when(jnp.logical_not(mine(e, half)))
            def _():
                hand(e, half).wait_send()

    @pl.loop(0, 32)
    def _(g):
        @pl.when(jnp.logical_not(is_self & (g == slot)))
        def _():
            pltpu.make_async_remote_copy(
                src_ref=part.at[0],
                dst_ref=final.at[g],
                send_sem=fs_sem.at[0, 0],
                recv_sem=fr_sem.at[g],
                device_id=((g // 4) * 4 + source_x, (g % 4) * 4 + source_y),
                device_id_type=MESH,
            ).wait_recv()

    total = final[0]
    for g in range(1, 32):
        total = total + final[g]
    total = jnp.where(my_half == 1, pltpu.roll(total, 124, 1), total)
    spread = jnp.where((lane & 7) == sub, jnp.broadcast_to(total, (8, 128)), 0.0)
    place = lax.broadcasted_iota(jnp.int32, (128, 128), 0) >> 3
    column = lax.broadcasted_iota(jnp.int32, (128, 128), 1)
    picked = jnp.dot(
        spread,
        jnp.where(place == column, 1.0, 0.0),
        precision=lax.Precision.HIGHEST,
        preferred_element_type=jnp.float32,
    )
    o_ref[0, 0] = picked[:4, :EV]
    o_ref[1, 0] = picked[:4, EV : 2 * EV]


def local(weights):
    vmem = pltpu.VMEM
    dma = pltpu.SemaphoreType.DMA
    out = pl.pallas_call(
        kernel,
        out_shape=jax.ShapeDtypeStruct((2, 1, 4, EV), jnp.float32),
        in_specs=[pl.BlockSpec(memory_space=pl.ANY)],
        out_specs=pl.BlockSpec(memory_space=vmem),
        scratch_shapes=[
            vmem((ROWS, 4, 8, 128), jnp.float32),
            vmem((16 * SLOT, 128), jnp.float32),
            vmem((16 * SLOT, 128), jnp.float32),
            vmem((ROWS, 16, 128), jnp.float32),
            vmem((ROWS, 16, 128), jnp.float32),
            vmem((ROWS, 8, 128), jnp.float32),
            vmem((ROWS, 8, 128), jnp.float32),
            vmem((NODES, 8, 128), jnp.float32),
            vmem((3, 58, 8, 128), jnp.float32),
            vmem((3, 2, 8, 128), jnp.int32),
            vmem((2, 16, 8, 128), jnp.float32),
            vmem((2, 8, 128), jnp.float32),
            vmem((2, 8, 128), jnp.float32),
            vmem((16, 1, 128), jnp.float32),
            vmem((32, 1, 128), jnp.float32),
            dma(()),
            dma((PHASES, 16)),
            dma((PHASES, 16)),
            dma((PHASES, 2)),
            pltpu.SemaphoreType.REGULAR((7,)),
            dma((2,)),
            dma((16, 2)),
            dma((32,)),
        ],
        compiler_params=pltpu.CompilerParams(
            collective_id=0, has_side_effects=True, vmem_limit_bytes=54784 * 1024
        ),
    )(weights.reshape(ROWS, 4, 8, 128))
    return jnp.transpose(out, (3, 0, 1, 2))


def solution(mesh):
    return jax.shard_map(
        local,
        mesh=mesh,
        in_specs=(P(None, None, "bx", "by", None),),
        out_specs=P(None, None, "bx", "by"),
        check_vma=False,
    )
```

```python
import functools
import math

import jax
import jax.numpy as jnp
import numpy as np
from jax import lax
from jax.experimental import pallas as pl
from jax.experimental.pallas import tpu as pltpu
from jax.sharding import PartitionSpec as P

N = 16384
P_SIZE = 5
LEVEL_BOXES = 128
EV = 8
NODES = P_SIZE * P_SIZE
ROWS = 2 * NODES
PHASES = 4
WIDE = 2
STRIDE = 32
SLOT = PHASES * STRIDE
MESH = pl.DeviceIdType.MESH

SIN = (4.44288292, -7.3082457, 3.60635441, -0.84611289, 0.10982699)
COS = (1.4142135, -6.97885099, 5.73946117, -1.88356299, 0.31069819)


def nodes():
    return np.cos(np.pi * (2.0 * np.arange(P_SIZE) + 1.0) / (2.0 * P_SIZE)) / 2.0


def lower_table():
    z = nodes()
    child = -0.25 + z / 2.0
    table = np.ones((P_SIZE, P_SIZE))
    for m in range(P_SIZE):
        for j in range(P_SIZE):
            if j != m:
                table[m] *= (child - z[j]) / (z[m] - z[j])
    return table


Z = [float(v) for v in nodes()]
LOW = lower_table()
POINTS = [((f + 0.5) / EV - 0.5, ((3 * f) % EV + 0.5) / EV - 0.5) for f in range(EV)]


def turn(theta):
    u = theta - jnp.round(theta)
    w = u * u
    s = SIN[4]
    c = COS[4]
    for k in (3, 2, 1, 0):
        s = s * w + SIN[k]
        c = c * w + COS[k]
    s = s * u
    return 1.0 - s * s, s * c


def interpolate_one(values, upper):
    values = [jnp.where(upper == 0, values[j], values[4 - j]) for j in range(5)]
    sign = (1 - 2 * upper).astype(jnp.float32)
    out = [None] * 5
    for m in (0, 1):
        a = sum_of(values, [0.5 * (LOW[m, j] + LOW[4 - m, j]) for j in range(5)])
        b = sum_of(values, [0.5 * (LOW[m, j] - LOW[4 - m, j]) for j in range(5)]) * sign
        out[m] = a + b
        out[4 - m] = a - b
    out[2] = sum_of(values, [LOW[2, j] for j in range(5)])
    return out


def interpolate(low, high):
    even = [low[j] + high[4 - j] for j in range(5)]
    odd = [low[j] - high[4 - j] for j in range(5)]
    out = [None] * 5
    for m in (0, 1):
        a = sum_of(even, [0.5 * (LOW[m, j] + LOW[4 - m, j]) for j in range(5)])
        b = sum_of(odd, [0.5 * (LOW[m, j] - LOW[4 - m, j]) for j in range(5)])
        out[m] = a + b
        out[4 - m] = a - b
    out[2] = sum_of(even, [LOW[2, j] for j in range(5)])
    return out


def sum_of(values, factors):
    total = None
    for v, f in zip(values, factors):
        if abs(f) < 1e-14:
            continue
        term = v * float(f)
        total = term if total is None else total + term
    return total


def speeds(x1, x2):
    cp, _ = turn(x1 - x2)
    cq, _ = turn(x1 + x2)
    return (2.0 + 0.5 * (cp - cq)) * 0.0625, (2.0 + 0.5 * (cp + cq)) * 0.0625


def moved(x1, x2, c1, c2, d1, d2, sign=None):
    dp, dq = d1 - d2, d1 + d2
    half = 0.5 if sign is None else 0.5 * sign
    _, sp = turn(x1 - x2 + half * dp)
    _, sq = turn(x1 + x2 + half * dq)
    gp = sp * (-2.0 * math.sin(math.pi * dp))
    gq = sq * (-2.0 * math.sin(math.pi * dq))
    e1 = (gp - gq) * 0.03125
    e2 = (gp + gq) * 0.03125
    if sign is not None:
        e1, e2 = e1 * sign, e2 * sign
    n1, n2 = c1 + e1, c2 + e2
    return n1 * n1, n2 * n2, e1 * (c1 + n1), e2 * (c2 + n2)


def root(s):
    return s * lax.rsqrt(s)


def inverse(s):
    return pltpu.reciprocal(s, approx=True)


def kernel(w_hbm, o_ref, w_ref, send, recv, st0, st1, st2, st3, norms, geo, lanes, acc, gift_out, gift_in, part, final,
           load_sem, send_sem, recv_sem, own_sem, far_sem, gift_sem, fs_sem, fr_sem):
    bx, by = lax.axis_index("bx"), lax.axis_index("by")
    gi, gj = bx // 4, by // 4
    b0, b1 = bx % 2, (bx // 2) % 2
    c0, c1 = by % 2, (by // 2) % 2
    me = b0 + 2 * c0 + 4 * b1 + 8 * c1
    mine_d = (16 - me) % 16
    slot = gi * 4 + gj
    source = (16 - (2 * gi + gj // 2)) % 16
    source_x, source_y = source % 2 + 2 * ((source // 4) % 2), (source // 2) % 2 + 2 * (source // 8)
    my_half = gj % 2
    is_self = source == me

    load = pltpu.make_async_copy(w_hbm, w_ref, load_sem)
    load.start()

    def peer(k):
        flip = lambda bit, at: (1 - bit) if (k >> at) & 1 else bit
        q0, r0, q1, r1 = flip(b0, 0), flip(c0, 1), flip(b1, 2), flip(c1, 3)
        return q0 + 2 * r0 + 4 * q1 + 8 * r1, (gi * 4 + q0 + 2 * q1, gj * 4 + r0 + 2 * r1)

    def flipped(at_x, at_y):
        def flip(v, bits):
            for size in (1, 2, 4, 8, 16):
                if bits & size:
                    v = v + size * (1 - 2 * ((v // size) % 2))
            return v

        return flip(bx, at_x), flip(by, at_y)

    near = [k for k in (4, 12, 5, 13, 8, 9, 1)]
    order = [k for k in range(16) if k & 2] + near

    steps_y = ((4, 0), (4, 1))
    steps_far = ((8, 0), (16, 0), (0, 4), (0, 12))
    barrier = pltpu.get_barrier_semaphore()
    for device in [peer(k)[1] for k in near] + [flipped(*at) for at in steps_y + steps_far]:
        pl.semaphore_signal(barrier, inc=1, device_id=device, device_id_type=MESH)

    def tell(n, at):
        pl.semaphore_signal(far_sem.at[n], inc=1, device_id=flipped(*at), device_id_type=MESH)

    def told(n):
        pl.semaphore_wait(far_sem.at[n], 1)

    lane = lax.broadcasted_iota(jnp.int32, (8, 128), 1)
    sub = lax.broadcasted_iota(jnp.int32, (8, 128), 0)
    bit = lambda v, at: (v >> at) & 1
    s2, s1, s0 = (bit(sub, at) for at in (2, 1, 0))
    l6, l5, l4, l3 = (bit(lane, at) for at in (6, 5, 4, 3))

    def shuffle(n):
        phase, t = n // NODES, n % NODES
        r = phase * STRIDE + t
        a = pltpu.roll(w_ref[t, phase], 0, 1, stride=8, stride_axis=0)
        b = pltpu.roll(w_ref[NODES + t, phase], 64, 1, stride=8, stride_axis=0)
        for by_row, l_bit in ((1, l3), (2, l4), (4, l5)):
            ra, rb = pltpu.roll(a, 8 - by_row, 0), pltpu.roll(b, 8 - by_row, 0)
            wraps = sub >= 8 - by_row
            go, wrap = (l_bit == 1) & jnp.logical_not(wraps), (l_bit == 1) & wraps
            a, b = jnp.where(go, ra, jnp.where(wrap, rb, a)), jnp.where(go, rb, jnp.where(wrap, ra, b))
        a, b = jnp.where(l6 == 1, b, a), jnp.where(l6 == 1, a, b)
        send[pl.ds(r, 8, stride=SLOT), :] = a
        send[pl.ds(8 * SLOT + r, 8, stride=SLOT), :] = b

    def exchange(p, k):
        start, count = p * STRIDE, NODES
        at, device = peer(k)
        place = me
        if p < WIDE:
            device = peer(k & 13)[1]
            place = b0 + (k & 2) + 4 * b1 + 8 * c1
        return pltpu.make_async_remote_copy(
            src_ref=send.at[pl.ds(pl.multiple_of(at * SLOT + start, 8), count)],
            dst_ref=recv.at[pl.ds(pl.multiple_of(place * SLOT + start, 8), count)],
            send_sem=send_sem.at[p, k],
            recv_sem=recv_sem.at[p, k],
            device_id=device,
            device_id_type=MESH,
        )

    def own(p, k):
        start, count = p * STRIDE, NODES
        at = peer(k)[0]
        place = b0 + k + 4 * b1 + 8 * c1 if p < WIDE else me
        return pltpu.make_async_copy(
            send.at[pl.ds(pl.multiple_of(at * SLOT + start, 8), count)],
            recv.at[pl.ds(pl.multiple_of(place * SLOT + start, 8), count)],
            own_sem.at[p, k // 2],
        )

    wide_order = [k | more for k in near for more in (0, 2)]
    orders = [wide_order if p < WIDE else order for p in range(PHASES)]
    owns = [(0, 2) if p < WIDE else (0,) for p in range(PHASES)]

    def pack(p):
        @pl.loop(0, 5)
        def _(g):
            for u in range(5):
                shuffle(p * NODES + g * 5 + u)

    def ship(p):
        for k in orders[p]:
            exchange(p, k).start()
        for k in owns[p]:
            own(p, k).start()

    load.wait()
    pack(0)
    pl.semaphore_wait(barrier, 13)
    tell(0, steps_y[0])
    tell(1, steps_y[1])
    for p in range(WIDE):
        if p > 0:
            pack(p)
        ship(p)
    told(0)
    told(1)
    tell(2, steps_y[1])
    for p in range(WIDE, PHASES):
        pack(p)
    told(2)
    ship(WIDE)
    tell(3, steps_far[0])

    f32 = lambda v: v.astype(jnp.float32)
    m2, m1, m0 = f32(s2) - 0.5, f32(s1) - 0.5, f32(s0) - 0.5
    h1, h2 = 1.0 / 256, 1.0 / 512
    steps = (0.5 * h1, 0.5 * h1, 0.5 * h2, 0.5 * h2)
    other_d = (16 - peer(2)[0]) % 16

    def lines(d):
        d = jnp.zeros_like(lane) + d
        source_row = ((lane >> 3) + (16 - d)) & 15
        line2 = 8 * (d & 1) + (lane & 7)
        xa1 = (f32((17 * (d >> 1) + 3) & 127) + 0.5) * (1.0 / 128)
        xa2 = (f32((29 * line2 + 11) & 127) + 0.5) * (1.0 / 128)
        return source_row & 7, source_row >> 3, xa1, xa2

    def center(index, width):
        return f32(index) * width + (0.5 * width - N / 2.0)

    def prepare(which, d, levels):
        box2, last, xa1, xa2 = lines(d)
        lanes[which, 0], lanes[which, 1] = box2, last
        m3 = f32(last) - 0.5
        places = (
            (xa1, xa2),
            (xa1 + m1 * h1, xa2),
            (xa1 + m0 * h1, xa2 + m1 * h1),
            (xa1 + m0 * h1 + m2 * h2, xa2 + m1 * h1),
            (xa1 + m0 * h1 + m2 * h2, xa2 + m1 * h1 + m3 * h2),
        )
        for level in levels:
            x, d = places[level], steps[level] if level < 4 else None
            c = speeds(*x)
            if level < 4:
                shift = (d, 0.0) if level % 2 == 0 else (0.0, d)
                sign = 2.0 * (m2 if level < 3 else m3)
                for n, v in enumerate((c[0] * c[0], c[1] * c[1]) + moved(*x, *c, *shift, sign)):
                    geo[which, 6 * level + n] = v
            else:
                geo[which, 24], geo[which, 25] = c[0] * c[0], c[1] * c[1]
                for f in range(EV):
                    for n, v in enumerate(moved(*x, *c, h2 * POINTS[f][0], h2 * POINTS[f][1])):
                        geo[which, 26 + 4 * f + n] = v

    def split(level, p, which, load, store, wide=False):
        box2, last = lanes[which, 0], lanes[which, 1]
        single = wide and level == 1
        below = c0 if wide else s0
        first = level == 0
        along = level % 2
        other = 1 - along
        if level == 0:
            index = [lambda c: p * 32 + 4 * gi + 2 * s1 + c, lambda c: box2 * 16 + 4 * gj + 2 * last + below]
            widths = (128.0, 128.0)
        elif level == 1:
            index = [lambda c: p * 16 + 2 * gi + s0, lambda c: box2 * 16 + 4 * gj + 2 * last + c]
            widths = (256.0, 128.0)
        elif level == 2:
            index = [lambda c: jnp.zeros_like(lane) + (p * 16 + 2 * gi + c), lambda c: box2 * 8 + 2 * gj + last]
            widths = (256.0, 256.0)
        else:
            index = [lambda c: jnp.zeros_like(lane) + (p * 8 + gi), lambda c: box2 * 8 + 2 * gj + c]
            widths = (512.0, 256.0)
        base, new, more = ((geo[which, 6 * level + n], geo[which, 6 * level + n + 1]) for n in (0, 2, 4))
        step = (2.0 * steps[level]) * (m2 if level < 3 else f32(last) - 0.5)
        x = lines(group(which))[2:] if first else None

        def table(dim, c):
            mid = center(index[dim](c), widths[dim])
            old, norm, diff, line = [], [], [], []
            for i in range(5):
                off = widths[dim] * Z[i]
                k = mid + off
                sq = k * k
                norm.append(new[dim] * sq)
                if first:
                    diff.append(more[dim] * sq + base[dim] * (off * (k + mid)))
                    line.append(step * mid + (x[dim] + step) * off if dim == along else x[dim] * off)
                else:
                    old.append(base[dim] * sq)
                    diff.append(more[dim] * sq)
                    line.append(step * k if dim == along else None)
            if first:
                old = base[dim] * (mid * mid)
            return old, norm, diff, line

        side = table(other, 0)
        children = (c0,) if single else (0, 1)
        main = [table(along, c) for c in children]
        fixed = [root(old + side[0]) for old, _, _, _ in main] if first else None
        for j in range(5):
            point = lambda i: (i * 5 + j) if along == 0 else (j * 5 + i)
            real, imag = [], []
            for c in range(len(children)):
                rr, ii = [], []
                old, norm, diff, line = main[c]
                for i in range(5):
                    here = fixed[c] if first else root(old[i] + side[0][j])
                    theta = line[i] + (diff[i] + side[2][j]) * inverse(root(norm[i] + side[1][j]) + here)
                    if first:
                        theta = theta + side[3][j]
                    cs, sn = turn(theta)
                    vr, vi = load(c, point(i))
                    rr.append(vr * cs - vi * sn)
                    ii.append(vr * sn + vi * cs)
                real.append(rr)
                imag.append(ii)
            for comp, terms in ((0, real), (1, imag)):
                out = interpolate_one(terms[0], c0) if single else interpolate(terms[0], terms[1])
                for i in range(5):
                    store(comp, point(i), out[i])

    def evaluate(p, which, src):
        box2 = lanes[which, 0]
        mid1 = center(jnp.zeros_like(lane) + (p * 8 + gi), 512.0)
        mid2 = center(box2 * 4 + gj, 512.0)
        k1 = [mid1 + 512.0 * z for z in Z]
        k2 = [mid2 + 512.0 * z for z in Z]
        sq1 = [k * k for k in k1]
        sq2 = [k * k for k in k2]
        for i in range(5):
            for j in range(5):
                norms[i * 5 + j] = root(geo[which, 24] * sq1[i] + geo[which, 25] * sq2[j])
        for f in range(EV):
            d1, d2 = h2 * POINTS[f][0], h2 * POINTS[f][1]
            a = [geo[which, 26 + 4 * f + n] for n in range(4)]
            n1, n2 = [a[0] * v for v in sq1], [a[1] * v for v in sq2]
            g1, g2 = [a[2] * v for v in sq1], [a[3] * v for v in sq2]
            line1, line2 = [d1 * k for k in k1], [d2 * k for k in k2]
            real, imag = acc[which, 2 * f], acc[which, 2 * f + 1]
            for i in range(5):
                for j in range(5):
                    t = i * 5 + j
                    theta = (line1[i] + line2[j]) + (g1[i] + g2[j]) * inverse(
                        root(n1[i] + n2[j]) + norms[t]
                    )
                    cs, sn = turn(theta)
                    vr, vi = src[t], src[NODES + t]
                    real = real + (vr * cs - vi * sn)
                    imag = imag + (vr * sn + vi * cs)
            acc[which, 2 * f], acc[which, 2 * f + 1] = real, imag

    def group(which):
        if which == 2:
            return jnp.where(s0 == 0, mine_d, other_d)
        return mine_d

    def arrived(p, which):
        last = lanes[which, 1]
        lower = sub < 4

        def load(c, t):
            v = recv[pl.ds(c * SLOT + p * STRIDE + t, 8, stride=2 * SLOT), :]
            turned = pltpu.roll(v, 4, 0)
            u0, u1 = jnp.where(lower, v, turned), jnp.where(lower, turned, v)
            return jnp.where(last == 0, u0, pltpu.roll(u1, 64, 1)), jnp.where(last == 0, pltpu.roll(u0, 64, 1), u1)

        return load

    def twice(dst):
        def store(q, t, v):
            dst[q * NODES + t, pl.ds(0, 8), :] = v
            dst[q * NODES + t, pl.ds(8, 8), :] = v

        return store

    def once(dst):
        def store(q, t, v):
            dst[q * NODES + t] = v

        return store

    def rest(p, which):
        last = lanes[which, 1]

        def held(c, t):
            return tuple(st1[q * NODES + t, pl.ds(c, 8, stride=2), :] for q in range(2))

        def across(c, t):
            v = [st2[q * NODES + t] for q in range(2)]
            return tuple(jnp.where(last == c, u, pltpu.roll(u, 64, 1)) for u in v)

        split(2, p, which, held, once(st2))
        split(3, p, which, across, once(st3))
        evaluate(p, which, st3)

    def fold(which, d):
        level = [pltpu.roll(acc[which, g], (16 - d) * 8, 1) for g in range(16)]
        for l_bit, by_lane in ((l5, 32), (l4, 16), (l3, 8)):
            count = len(level) // 2
            merged = []
            for g in range(count):
                u, v = level[g], level[g + count]
                keep = jnp.where(l_bit == 0, u, v)
                give = jnp.where(l_bit == 0, v, u)
                merged.append(
                    keep + jnp.where(l_bit == 0, pltpu.roll(give, 128 - by_lane, 1), pltpu.roll(give, by_lane, 1))
                )
            level = merged
        level = [v * (1.0 / (P_SIZE * LEVEL_BOXES)) for v in level]
        return (
            jnp.where(l6 == 0, level[0], pltpu.roll(level[1], 64, 1)),
            jnp.where(l6 == 0, pltpu.roll(level[0], 64, 1), level[1]),
        )

    acc[...] = jnp.zeros_like(acc)
    prepare(2, group(2), (0,))
    prepare(0, mine_d, range(5))
    prepare(1, other_d, range(1, 5))

    def await_piece(q):
        for k in owns[q]:
            own(q, k).wait()
        for k in orders[q]:
            exchange(q, k).wait_recv()

    @pl.loop(0, WIDE)
    def _(p):
        for q in range(WIDE):

            @pl.when(p == q)
            def _():
                await_piece(q)
                told(3 + q)
                tell(4 + q, steps_far[1 + q])

        split(0, p, 2, arrived(p, 2), twice(st0), wide=True)

        @pl.when(p == 0)
        def _():
            for q in range(WIDE + 1, PHASES):
                ship(q)

        @pl.loop(0, 2)
        def _(which):
            def side(c, t):
                return tuple(st0[q * NODES + t, pl.ds(which, 8, stride=2), :] for q in range(2))

            split(1, p, which, side, twice(st1), wide=True)
            rest(p, which)

    gift = pltpu.make_async_remote_copy(
        src_ref=gift_out,
        dst_ref=gift_in,
        send_sem=gift_sem.at[0],
        recv_sem=gift_sem.at[1],
        device_id=flipped(0, 1),
        device_id_type=MESH,
    )
    gift_out[0], gift_out[1] = fold(1, other_d)
    gift.start()
    told(5)
    tell(6, steps_far[3])

    @pl.loop(WIDE, PHASES)
    def _(p):
        for q in range(WIDE, PHASES):

            @pl.when(p == q)
            def _():
                await_piece(q)

        def held(c, t):
            return tuple(st0[q * NODES + t, pl.ds(c, 8, stride=2), :] for q in range(2))

        split(0, p, 0, arrived(p, 0), twice(st0))
        split(1, p, 0, held, twice(st1))
        rest(p, 0)

    told(6)
    gift.wait()
    totals = fold(0, mine_d)
    for h in range(2):
        total = totals[h] + gift_in[h]
        for e in range(8):
            part[8 * h + e] = total[e : e + 1, :]

    line1 = mine_d // 2

    def hand(e, half):
        e4, e3, e2, e1 = (e >> 3) & 1, (e >> 2) & 1, (e >> 1) & 1, e & 1
        return pltpu.make_async_remote_copy(
            src_ref=part.at[e],
            dst_ref=final.at[slot],
            send_sem=fs_sem.at[e, half],
            recv_sem=fr_sem.at[slot],
            device_id=(4 * line1 + 2 * e3 + e1, 4 * (2 * (mine_d % 2) + half) + 2 * e4 + e2),
            device_id_type=MESH,
        )

    def mine(e, half):
        return is_self & (me == e) & (my_half == half)

    for e in range(16):
        for half in range(2):

            @pl.when(jnp.logical_not(mine(e, half)))
            def _():
                hand(e, half).start()

    @pl.when(is_self)
    def _():
        final[slot] = part[me]

    for p in range(PHASES):
        for k in orders[p]:
            exchange(p, k).wait_send()

    for e in range(16):
        for half in range(2):

            @pl.when(jnp.logical_not(mine(e, half)))
            def _():
                hand(e, half).wait_send()

    @pl.loop(0, 32)
    def _(g):
        @pl.when(jnp.logical_not(is_self & (g == slot)))
        def _():
            pltpu.make_async_remote_copy(
                src_ref=part.at[0],
                dst_ref=final.at[g],
                send_sem=fs_sem.at[0, 0],
                recv_sem=fr_sem.at[g],
                device_id=((g // 4) * 4 + source_x, (g % 4) * 4 + source_y),
                device_id_type=MESH,
            ).wait_recv()

    total = final[0]
    for g in range(1, 32):
        total = total + final[g]
    total = jnp.where(my_half == 1, pltpu.roll(total, 124, 1), total)
    spread = jnp.where((lane & 7) == sub, jnp.broadcast_to(total, (8, 128)), 0.0)
    place = lax.broadcasted_iota(jnp.int32, (128, 128), 0) >> 3
    column = lax.broadcasted_iota(jnp.int32, (128, 128), 1)
    picked = jnp.dot(
        spread,
        jnp.where(place == column, 1.0, 0.0),
        precision=lax.Precision.HIGHEST,
        preferred_element_type=jnp.float32,
    )
    o_ref[0, 0] = picked[:4, :EV]
    o_ref[1, 0] = picked[:4, EV : 2 * EV]


def local(weights):
    vmem = pltpu.VMEM
    dma = pltpu.SemaphoreType.DMA
    out = pl.pallas_call(
        kernel,
        out_shape=jax.ShapeDtypeStruct((2, 1, 4, EV), jnp.float32),
        in_specs=[pl.BlockSpec(memory_space=pl.ANY)],
        out_specs=pl.BlockSpec(memory_space=vmem),
        scratch_shapes=[
            vmem((ROWS, 4, 8, 128), jnp.float32),
            vmem((16 * SLOT, 128), jnp.float32),
            vmem((16 * SLOT, 128), jnp.float32),
            vmem((ROWS, 16, 128), jnp.float32),
            vmem((ROWS, 16, 128), jnp.float32),
            vmem((ROWS, 8, 128), jnp.float32),
            vmem((ROWS, 8, 128), jnp.float32),
            vmem((NODES, 8, 128), jnp.float32),
            vmem((3, 58, 8, 128), jnp.float32),
            vmem((3, 2, 8, 128), jnp.int32),
            vmem((2, 16, 8, 128), jnp.float32),
            vmem((2, 8, 128), jnp.float32),
            vmem((2, 8, 128), jnp.float32),
            vmem((16, 1, 128), jnp.float32),
            vmem((32, 1, 128), jnp.float32),
            dma(()),
            dma((PHASES, 16)),
            dma((PHASES, 16)),
            dma((PHASES, 2)),
            pltpu.SemaphoreType.REGULAR((7,)),
            dma((2,)),
            dma((16, 2)),
            dma((32,)),
        ],
        compiler_params=pltpu.CompilerParams(
            collective_id=0, has_side_effects=True, vmem_limit_bytes=54784 * 1024
        ),
    )(weights.reshape(ROWS, 4, 8, 128))
    return jnp.transpose(out, (3, 0, 1, 2))


def solution(mesh):
    return jax.shard_map(
        local,
        mesh=mesh,
        in_specs=(P(None, None, "bx", "by", None),),
        out_specs=P(None, None, "bx", "by"),
        check_vma=False,
    )
```
